768 devices in a mesh: row: 16 (over x, y_hi), col: 48 (over z, y_lo, core).
Axes of the slice: x: 4, y: 8 (y_hi: 4, y_lo: 2; y = y_hi * 2 + y_lo), z: 12, core: 2. Of those that a mesh axis runs over, the one named last changes fastest.
Arguments:
- p_blocks: bfloat16 [64, 48, 128, 128], P('row', 'col'), may hold values from -0.29882812 to 0.29882812
- p_cols: int32 [64, 48], P('row', 'col'), may hold values from -1 to 767, as said below
- h_blocks: bfloat16 [32, 96, 128, 128], P('row', 'col'), may hold values from -3 to 3
- h_rows: int32 [32, 96], P('row', 'col'), may hold values from -1 to 767, as said below
- keep: int32 [64, 96], P('row', 'col'), may hold values 0 or 1
Outputs:
- product: bfloat16 [64, 96, 128, 128], P('row', 'col')
The draws below stay inside these ranges and needn't reach their ends.
Inputs may be any that keep to these rules, and one draw needn't show every extreme that they name: `p_cols`: entry (i, c) is -1 or a block column from c * 16 to c * 16 + 15. `h_rows`: entry (t, j) is -1 or a block row from r * 48 to r * 48 + 47, where r = t // 2; the entries of one block column that are not -1 are distinct.
All inputs are finite; a program needn't handle non-finite values. No bound on the sum of `keep` on one device may be relied on, other than what follows from the above.
Results may differ from the reference program's by a relative error of at most 0.001.
Values may be sent and summed in bfloat16 or wider, within the bound.
A program may use at most 64 MiB of HBM per device.

```python
import jax
import jax.numpy as jnp
from jax import lax

BS = 128
RB = 4
JB = 2
SH = 2
ROWS_ALL = 64
COLS_ALL = 96
H_SLOTS = 32
N_ROW = 16
N_COL = 48


def active_offsets(key):
    range_keys = jax.random.split(key, N_COL)
    orders = jax.vmap(lambda range_key: jax.random.permutation(range_key, N_ROW))(range_keys)
    return orders[:, :2].astype(jnp.int32)


def draw_p_cols(key, part):
    offsets = active_offsets(key)
    key = jax.random.fold_in(key, 11)
    pick_key, rate_key, live_key = jax.random.split(key, 3)
    row_count = RB * N_ROW
    choose = jax.random.randint(pick_key, (row_count, N_COL), 0, 2)
    rates = jax.random.randint(rate_key, (row_count, 1), 2, 9)
    alive = jax.random.randint(live_key, (row_count, N_COL), 0, 8) < rates
    ranges = jnp.arange(N_COL, dtype=jnp.int32)[None, :]
    chosen = jnp.where(choose == 0, offsets[:, 0][None, :], offsets[:, 1][None, :])
    return jnp.where(alive, ranges * N_ROW + chosen, -1).astype(jnp.int32)


def draw_h_rows(key, part):
    offsets = active_offsets(key)
    key = jax.random.fold_in(key, 12)
    order_key, live_key = jax.random.split(key)
    group = N_COL // N_ROW
    column_total = JB * N_COL
    orders = jax.vmap(lambda one_key: jax.random.permutation(one_key, 2 * group))(jax.random.split(order_key, N_ROW * column_total))
    chosen = orders[:, :SH].reshape(N_ROW, column_total, SH).astype(jnp.int32)
    row_index = jnp.arange(N_ROW, dtype=jnp.int32)[:, None, None]
    range_index = row_index * group + chosen // 2
    offset = offsets[range_index, chosen % 2]
    block_row = range_index * N_ROW + offset
    alive = jax.random.randint(live_key, block_row.shape, 0, 4) >= 1
    values = jnp.where(alive, block_row, -1)
    return jnp.transpose(values, (0, 2, 1)).reshape(SH * N_ROW, column_total).astype(jnp.int32)


def plant(array, stream_key, low, top_value):
    spot = [jax.random.randint(jax.random.fold_in(stream_key, axis), (), 0, length) for axis, length in enumerate(array.shape)]
    main_axis = array.shape.index(max(array.shape))
    beside = spot[:main_axis] + [(spot[main_axis] + 1) % array.shape[main_axis]] + spot[main_axis + 1:]
    return array.at[tuple(spot)].set(low).at[tuple(beside)].set(top_value)


def block_levels(key, dims, pieces, low, top_value):
    def one(axis_at, shards_of):
        draws = jax.random.uniform(jax.random.fold_in(jax.random.fold_in(key, 6), axis_at), (shards_of,), jnp.float32, low / len(pieces), top_value / len(pieces))
        return jnp.repeat(jnp.exp(draws), dims[axis_at] // shards_of).reshape((-1,) + (1,) * (len(dims) - axis_at - 1))

    gain = one(*pieces[0])
    for cut in pieces[1:]:
        gain = gain * one(*cut)
    return gain


def scatter_about(own_key, extent, width, reach, pieces=(), held_as=jnp.bfloat16):
    values = jax.random.normal(own_key, extent, jnp.float32) * width
    if len(pieces) > 0:
        values = block_levels(own_key, extent, pieces, -0.22, 0.18) * values
    return jnp.clip(values, min=-reach, max=reach).astype(held_as)


def setup_inputs(seed: int = 0) -> dict:
    streams_of = jax.random.split(jax.random.key(seed), 6)
    p_blocks = scatter_about(streams_of[0], (ROWS_ALL, N_COL, BS, BS), 0.044, 0.29882812, ((0, 16), (1, 48)))
    p_cols = draw_p_cols(jax.random.fold_in(streams_of[5], 71), 0)
    h_blocks = scatter_about(streams_of[2], (H_SLOTS, COLS_ALL, BS, BS), 0.5, 3.0, ((0, 16), (1, 48)))
    h_rows = draw_h_rows(jax.random.fold_in(streams_of[5], 71), 0)
    keep = plant((jax.random.randint(streams_of[4], (ROWS_ALL, COLS_ALL), 0, 4) < 3).astype(jnp.int32), jax.random.fold_in(streams_of[4], 1), 0, 1)
    return dict(p_blocks=p_blocks, p_cols=p_cols, h_blocks=h_blocks, h_rows=h_rows, keep=keep)


def reference(p_blocks, p_cols, h_blocks, h_rows, keep):
    slot_count = h_rows.shape[0]

    def one_row(row_id):
        row_cols = p_cols[row_id]
        row_blocks = p_blocks[row_id]

        def one_column(col_id):
            column_rows = h_rows[:, col_id]
            column_blocks = h_blocks[:, col_id]

            def step(running, slot_id):
                block_row = column_rows[slot_id]
                range_id = jnp.clip(block_row // N_ROW, 0, N_COL - 1).astype(jnp.int32)
                usable = (block_row >= 0) & (row_cols[range_id] == block_row)

                def add_term(current):
                    return current + jnp.dot(row_blocks[range_id], column_blocks[slot_id], preferred_element_type=jnp.float32)

                return lax.cond(usable, add_term, lambda current: current, running), None

            summed, _ = lax.scan(step, jnp.zeros((BS, BS), jnp.float32), jnp.arange(slot_count, dtype=jnp.int32))
            return summed

        return lax.map(one_column, jnp.arange(h_rows.shape[1], dtype=jnp.int32))

    product_sum = lax.map(one_row, jnp.arange(p_cols.shape[0], dtype=jnp.int32))
    kept = jnp.where((keep == 1)[:, :, None, None], product_sum, jnp.zeros((), jnp.float32))
    return kept.astype(jnp.bfloat16)
```

```python
import jax
import jax.numpy as jnp
from jax import lax
from jax.experimental import pallas as pl
from jax.experimental.pallas import tpu as pltpu
from jax.sharding import PartitionSpec as P

BS = 128
NX, NYH, NZ, NYL, NC = 4, 4, 12, 2, 2
ROWS = 4 * BS
META = 16
FULL = ROWS + META
SPLIT = 304
MESH = pl.DeviceIdType.MESH

ORDER = [
    ("M", 0), ("A", 0), ("F", -1), ("F", 1), ("H", -1, 0), ("H", 1, 0), ("H", 0, -1), ("H", 0, 1),
    ("B", 0), ("M", -1), ("M", 1), ("A", -1), ("A", 1), ("N", 0), ("B", -1), ("H", -2, 0),
    ("H", 1, -1), ("N", -1), ("B", 1), ("H", 0, -2), ("F", -2), ("F", 2), ("N", 1), ("A", -2),
    ("A", 2), ("M", -2), ("H", -1, -1), ("H", 1, 1), ("M", 2), ("B", -2), ("F", -3), ("F", 3),
    ("H", -1, 1), ("N", -2), ("B", 2), ("H", 1, -2), ("A", -3), ("A", 3), ("M", -3), ("M", 3),
    ("N", 2), ("B", -3), ("H", -1, -2), ("F", -4), ("F", 4), ("N", -3), ("B", 3), ("A", -4),
    ("A", 4), ("H", -2, -1), ("M", -4), ("M", 4), ("N", 3), ("B", -4), ("F", -5), ("F", 5),
    ("H", -2, 1), ("N", -4), ("B", 4), ("A", -5), ("A", 5), ("M", -5), ("M", 5), ("H", -2, -2),
    ("N", 4), ("C", 4), ("B", -5), ("F", -6), ("A", 6), ("N", -5), ("B", 5), ("M", -6), ("N", 5),
    ("C", 5), ("B", -6), ("N", -6), ("C", 6),
]
KINDS = {"F": 0, "A": 12, "B": 24, "M": 36, "N": 48}
SEMS = 76


def sem_index(event):
    if event[0] == "H":
        return 60 + (event[1] % 4) * 4 + event[2] % 4
    return KINDS[event[0]] + event[1] % 12


def kernel(p_ref, pc_ref, h_ref, hr_ref, keep_ref, out_ref, pbuf, hbuf, lhs, acc, send_sem, recv_sem, own_sem):
    row, col = lax.axis_index("row"), lax.axis_index("col")
    x, yh = row // NYH, row % NYH
    z, yl, core = col // 4, (col // 2) % 2, col % 2
    sign = 1 - 2 * core

    def col_of(dz, flip_pair, flip_core):
        zz = (z + sign * dz + 2 * NZ) % NZ
        return zz * 4 + (1 - yl if flip_pair else yl) * 2 + (1 - core if flip_core else core)

    def row_of(dx, dy):
        return ((x + sign * dx + 2 * NX) % NX) * NYH + (yh + sign * dy + 2 * NYH) % NYH

    links = {
        "zp": (row, col_of(1, False, False)),
        "zm": (row, col_of(-1, False, False)),
        "y": (row, col_of(0, True, False)),
        "m": (row, col_of(0, False, True)),
        "xp": (row_of(1, 0), col),
        "xm": (row_of(-1, 0), col),
        "hp": (row_of(0, 1), col),
        "hm": (row_of(0, -1), col),
    }

    def region(event):
        kind = event[0]
        if kind == "H":
            return hbuf.at[row_of(event[1], event[2])]
        d = event[1]
        if kind == "F":
            return pbuf.at[col_of(d, False, False)]
        if kind == "A":
            return pbuf.at[col_of(d, True, False), pl.ds(0, SPLIT)]
        if kind == "B":
            return pbuf.at[col_of(d, True, False), pl.ds(SPLIT, FULL - SPLIT)]
        if kind == "M":
            return pbuf.at[col_of(-d, False, True)]
        return pbuf.at[col_of(-d, True, True)]

    barrier = pltpu.get_barrier_semaphore()
    for device in links.values():
        pl.semaphore_signal(barrier, inc=1, device_id=device, device_id_type=MESH)

    own_p, own_h = pbuf.at[col], hbuf.at[row]
    copy_p = pltpu.make_async_copy(p_ref, pbuf.at[col, pl.ds(0, ROWS)], own_sem.at[0])
    copy_h = pltpu.make_async_copy(h_ref, hbuf.at[row, pl.ds(0, ROWS)], own_sem.at[1])
    copy_p.start()
    copy_h.start()
    line = lax.broadcasted_iota(jnp.int32, (META, BS), 0)
    p_meta = jnp.zeros((META, BS), jnp.int32)
    h_meta = jnp.zeros((META, BS), jnp.int32)
    base = 48 * (col // 3)
    for i in range(4):
        value = pc_ref[i, 0]
        p_meta = jnp.where(line // 4 == i, jnp.where(value < 0, -1, value - base), p_meta)
        value = hr_ref[i // 2, i % 2]
        h_meta = jnp.where(line % 4 == i, jnp.where(value < 0, -2, value - 48 * row), h_meta)
    pbuf[col, pl.ds(ROWS, META), :] = p_meta.astype(jnp.float32).astype(jnp.bfloat16)
    hbuf[row, pl.ds(ROWS, META), :] = h_meta.astype(jnp.float32).astype(jnp.bfloat16)
    copy_p.wait()
    copy_h.wait()
    pl.semaphore_wait(barrier, len(links))

    sent = []

    def send(link, source, event):
        copy = pltpu.make_async_remote_copy(
            src_ref=source,
            dst_ref=source,
            send_sem=send_sem.at[len(sent)],
            recv_sem=recv_sem.at[sem_index(event)],
            device_id=links[link],
            device_id_type=MESH,
        )
        copy.start()
        sent.append(copy)

    def receive(event):
        here = region(event)
        pltpu.make_async_remote_copy(
            src_ref=here,
            dst_ref=here,
            send_sem=send_sem.at[0],
            recv_sem=recv_sem.at[sem_index(event)],
            device_id=links["m"],
            device_id_type=MESH,
        ).wait_recv()
        return here

    first = pbuf.at[col, pl.ds(0, SPLIT)]
    second = pbuf.at[col, pl.ds(SPLIT, FULL - SPLIT)]
    send("y", first, ("A", 0))
    send("zp", own_p, ("F", -1))
    send("zm", own_p, ("F", 1))
    send("hp", own_h, ("H", 0, -1))
    send("hm", own_h, ("H", 0, 1))
    send("xp", own_h, ("H", -1, 0))
    send("xm", own_h, ("H", 1, 0))
    send("y", second, ("B", 0))
    send("m", own_p, ("M", 0))

    def block_row(step, carry):
        r = step % 16
        h_tags = hbuf[r, pl.ds(ROWS, META), :].astype(jnp.float32)
        tags = []
        for u in range(3):
            p_tags = pbuf[3 * r + u, pl.ds(ROWS, META), :].astype(jnp.float32)
            tags.append(jnp.where(p_tags == h_tags, 1.0, 0.0))
        for i in range(4):
            blocks = [pbuf[3 * r + u, pl.ds(i * BS, BS), :] for u in range(3)]
            for q in range(4):
                picked = None
                for u in range(3):
                    tag = jnp.broadcast_to(tags[u][4 * i + q : 4 * i + q + 1, :], (BS, BS))
                    term = blocks[u] * tag.astype(jnp.bfloat16)
                    picked = term if picked is None else picked + term
                lhs[q % 2, pl.ds(i * BS, BS), pl.ds((q // 2) * BS, BS)] = picked
        for j in range(2):
            rhs = jnp.concatenate(
                [hbuf[r, pl.ds(j * BS, BS), :], hbuf[r, pl.ds((2 + j) * BS, BS), :]], axis=0
            )
            acc[j] += jnp.dot(lhs[j], rhs, preferred_element_type=jnp.float32)
        return carry

    def low(s):
        return (4 * (z + NZ - s) + 2) // 3

    def high(s):
        return (4 * (z + NZ + s + 1)) // 3

    acc[...] = jnp.zeros_like(acc)
    done = None
    have = set()
    for event in ORDER:
        kind = event[0]
        if kind == "C":
            s = event[1]
            if s < 6:
                edges = (low(s), high(s))
            else:
                edges = (high(done[2]) - 16, low(done[2]) + 16)
            if done is None:
                lax.fori_loop(edges[0], edges[1], block_row, 0)
            elif s < 6:
                lax.fori_loop(edges[0], done[0], block_row, 0)
                lax.fori_loop(done[1], edges[1], block_row, 0)
            else:
                lax.fori_loop(done[1], done[0] + 16, block_row, 0)
            done = edges + (s,)
            continue
        here = receive(event)
        d = event[1]
        if kind == "F":
            if -6 < d < 0:
                send("zp", here, ("F", d - 1))
            if 0 < d < 5:
                send("zm", here, ("F", d + 1))
            place = col_of(d, False, False)
            send("y", pbuf.at[place, pl.ds(SPLIT, FULL - SPLIT)], ("B", d))
            send("m", here, ("M", d))
        elif kind in "AB":
            if kind == "A" and -5 < d <= 0:
                send("zp", here, ("A", d - 1))
            if kind == "A" and 0 <= d < 6:
                send("zm", here, ("A", d + 1))
            have.add((kind, d % 12))
            if ("A", d % 12) in have and ("B", d % 12) in have:
                send("m", pbuf.at[col_of(d, True, False)], ("N", d))
        elif kind == "H":
            dy = event[2]
            if d == 0:
                if dy == -1:
                    send("hp", here, ("H", 0, -2))
                send("xp", here, ("H", -1, dy))
                send("xm", here, ("H", 1, dy))
            elif d == -1:
                send("xp", here, ("H", -2, dy))

    for i in range(4):
        for j in range(2):
            total = acc[j, pl.ds(i * BS, BS), :]
            kept = jnp.where(keep_ref[i, j] == 1, total, jnp.zeros_like(total))
            out_ref[i, j] = kept.astype(out_ref.dtype)
    for copy in sent:
        copy.wait_send()


def shards(p_blocks, p_cols, h_blocks, h_rows, keep):
    smem = pl.BlockSpec(memory_space=pltpu.SMEM)
    anywhere = pl.BlockSpec(memory_space=pl.ANY)
    return pl.pallas_call(
        kernel,
        out_shape=jax.ShapeDtypeStruct((4, 2, BS, BS), jnp.bfloat16),
        in_specs=[anywhere, smem, anywhere, smem, smem],
        out_specs=pl.BlockSpec(memory_space=pltpu.VMEM),
        scratch_shapes=[
            pltpu.VMEM((NZ * 4, FULL, BS), jnp.bfloat16),
            pltpu.VMEM((NX * NYH, FULL, BS), jnp.bfloat16),
            pltpu.VMEM((2, ROWS, 2 * BS), jnp.bfloat16),
            pltpu.VMEM((2, ROWS, BS), jnp.float32),
            pltpu.SemaphoreType.DMA((SEMS,)),
            pltpu.SemaphoreType.DMA((SEMS,)),
            pltpu.SemaphoreType.DMA((2,)),
        ],
        compiler_params=pltpu.CompilerParams(
            collective_id=0, has_side_effects=True, vmem_limit_bytes=24 * 1024 * 1024
        ),
        name="filtered_product",
    )(p_blocks.reshape(ROWS, BS), p_cols, h_blocks.reshape(ROWS, BS), h_rows, keep)


def solution(mesh):
    return jax.shard_map(
        shards,
        mesh=mesh,
        in_specs=(
            P("row", "col", None, None),
            P("row", "col"),
            P("row", "col", None, None),
            P("row", "col"),
            P("row", "col"),
        ),
        out_specs=P("row", "col", None, None),
        check_vma=False,
    )
```

```python
import jax
import jax.numpy as jnp
from jax import lax
from jax.experimental import pallas as pl
from jax.experimental.pallas import tpu as pltpu
from jax.sharding import PartitionSpec as P

BS = 128
NX, NYH, NZ, NYL, NC = 4, 4, 12, 2, 2
ROWS = 4 * BS
META = 16
FULL = ROWS + META
SPLIT = 288
LAG = 41
MESH = pl.DeviceIdType.MESH

ORDER = [
    ("M", 0), ("E", -1), ("E", 1), ("A", 0), ("H", -1, 0), ("G", -1), ("G", 1), ("H", 1, 0), ("M", -1),
    ("E", -2), ("E", 2), ("M", 1), ("A", -1), ("H", 0, -1), ("H", -2, 0), ("A", 1), ("G", -2), ("G", 2),
    ("M", -2), ("E", -3), ("H", 0, 1), ("B", 0), ("E", 3), ("M", 2), ("H", -1, -1), ("A", -2), ("B", -1),
    ("N", 0), ("A", 2), ("H", 1, -1), ("G", -3), ("B", 1), ("N", -1), ("G", 3), ("H", -1, 1), ("M", -3),
    ("E", -4), ("B", -2), ("N", 1), ("E", 4), ("M", 3), ("H", 1, 1), ("B", 2), ("A", -3), ("N", -2), ("A", 3),
    ("H", -2, -1), ("N", 2), ("G", -4), ("G", 4), ("H", -2, 1), ("M", -4), ("E", -5), ("H", 0, -2), ("E", 5),
    ("M", 4), ("B", -3), ("A", -4), ("C", 2, 0), ("A", 4), ("B", 3), ("N", -3), ("G", -5), ("B", -4),
    ("G", 5), ("N", 3), ("H", -1, -2), ("M", -5), ("E", -6), ("B", 4), ("N", -4), ("A", -5), ("M", 5),
    ("H", 1, -2), ("A", 5), ("B", -5), ("N", 4), ("G", -6), ("C", 4, 1), ("B", 5), ("N", -5), ("H", -2, -2),
    ("M", -6), ("B", -6), ("A", 6), ("C", 4, 2), ("N", 5), ("N", 6), ("C", 6, 2),
]
FIRST = [
    ("y", ("A", 0)),
    ("zp", ("E", -1)),
    ("zm", ("E", 1)),
    ("zp", ("G", -1)),
    ("zm", ("G", 1)),
    ("hp", ("H", 0, -1)),
    ("hm", ("H", 0, 1)),
    ("xp", ("H", -1, 0)),
    ("xm", ("H", 1, 0)),
    ("y", ("B", 0)),
    ("m", ("M", 0)),
]
KINDS = {"E": 0, "A": 12, "B": 24, "M": 36, "N": 48, "G": 60}
SEMS = 88


def sem_index(event):
    if event[0] == "H":
        return 72 + (event[1] % 4) * 4 + event[2] % 4
    return KINDS[event[0]] + event[1] % 12


def kernel(
    p_ref, pc_hbm, h_ref, hr_hbm, keep_hbm, out_ref,
    pbuf, hbuf, lhs, acc, pc_ref, hr_ref, keep_ref, send_sem, recv_sem, own_sem,
):
    row, col = lax.axis_index("row"), lax.axis_index("col")
    x, yh = row // NYH, row % NYH
    z, yl, core = col // 4, (col // 2) % 2, col % 2
    sign = 1 - 2 * core

    def col_of(dz, flip_pair, flip_core):
        zz = (z + sign * dz + 2 * NZ) % NZ
        return zz * 4 + (1 - yl if flip_pair else yl) * 2 + (1 - core if flip_core else core)

    def row_of(dx, dy):
        return ((x + sign * dx + 2 * NX) % NX) * NYH + (yh + sign * dy + 2 * NYH) % NYH

    links = {
        "zp": (row, col_of(1, False, False)),
        "zm": (row, col_of(-1, False, False)),
        "y": (row, col_of(0, True, False)),
        "m": (row, col_of(0, False, True)),
        "xp": (row_of(1, 0), col),
        "xm": (row_of(-1, 0), col),
        "hp": (row_of(0, 1), col),
        "hm": (row_of(0, -1), col),
    }
    head, tail = pl.ds(0, SPLIT), pl.ds(SPLIT, FULL - SPLIT)

    def region(event):
        kind, d = event[0], event[1]
        if kind == "H":
            return hbuf.at[row_of(d, event[2])]
        if kind == "E":
            return pbuf.at[col_of(d, False, False), tail]
        if kind == "G":
            return pbuf.at[col_of(d, False, False), head]
        if kind == "A":
            return pbuf.at[col_of(d, True, False), head]
        if kind == "B":
            return pbuf.at[col_of(d, True, False), tail]
        if kind == "M":
            return pbuf.at[col_of(-d, False, True)]
        return pbuf.at[col_of(-d, True, True)]

    barrier = pltpu.get_barrier_semaphore()
    for device in links.values():
        pl.semaphore_signal(barrier, inc=1, device_id=device, device_id_type=MESH)

    own = [
        pltpu.make_async_copy(pc_hbm, pc_ref, own_sem.at[0]),
        pltpu.make_async_copy(hr_hbm, hr_ref, own_sem.at[1]),
        pltpu.make_async_copy(keep_hbm, keep_ref, own_sem.at[2]),
        pltpu.make_async_copy(p_ref, pbuf.at[col, pl.ds(0, ROWS)], own_sem.at[3]),
        pltpu.make_async_copy(h_ref, hbuf.at[row, pl.ds(0, ROWS)], own_sem.at[4]),
    ]
    for copy in own:
        copy.start()
    acc[...] = jnp.zeros_like(acc)
    own[0].wait()
    own[1].wait()
    line = lax.broadcasted_iota(jnp.int32, (META, BS), 0)
    p_meta = jnp.zeros((META, BS), jnp.int32)
    h_meta = jnp.zeros((META, BS), jnp.int32)
    base = 48 * (col // 3)
    for i in range(4):
        value = pc_ref[0, i]
        p_meta = jnp.where(line // 4 == i, jnp.where(value < 0, -1, value - base), p_meta)
        value = hr_ref[i // 2, i % 2]
        h_meta = jnp.where(line % 4 == i, jnp.where(value < 0, -2, value - 48 * row), h_meta)
    pbuf[col, pl.ds(ROWS, META), :] = p_meta.astype(jnp.float32).astype(jnp.bfloat16)
    hbuf[row, pl.ds(ROWS, META), :] = h_meta.astype(jnp.float32).astype(jnp.bfloat16)
    for copy in own[2:]:
        copy.wait()
    pl.semaphore_wait(barrier, len(links))

    sent = []

    def send(link, source, event):
        copy = pltpu.make_async_remote_copy(
            src_ref=source,
            dst_ref=source,
            send_sem=send_sem.at[len(sent)],
            recv_sem=recv_sem.at[sem_index(event)],
            device_id=links[link],
            device_id_type=MESH,
        )
        copy.start()
        sent.append(copy)

    def receive(event):
        here = region(event)
        pltpu.make_async_remote_copy(
            src_ref=here,
            dst_ref=here,
            send_sem=send_sem.at[0],
            recv_sem=recv_sem.at[sem_index(event)],
            device_id=links["m"],
            device_id_type=MESH,
        ).wait_recv()
        return here

    own_part = {"A": pbuf.at[col, head], "G": pbuf.at[col, head], "B": pbuf.at[col, tail], "E": pbuf.at[col, tail]}
    own_part.update({"M": pbuf.at[col], "H": hbuf.at[row]})
    for link, event in FIRST:
        send(link, own_part[event[0]], event)

    def block_row(r):
        h_tags = hbuf[r, pl.ds(ROWS, META), :].astype(jnp.float32)
        tags = []
        for u in range(3):
            p_tags = pbuf[3 * r + u, pl.ds(ROWS, META), :].astype(jnp.float32)
            tags.append(jnp.where(p_tags == h_tags, 1.0, 0.0))
        left = [[[None, None] for _ in range(4)] for _ in range(2)]
        for i in range(4):
            blocks = [pbuf[3 * r + u, pl.ds(i * BS, BS), :].reshape(8, META, BS) for u in range(3)]
            for q in range(4):
                picked = jnp.zeros_like(blocks[0])
                for u in range(3):
                    tag = jnp.broadcast_to(tags[u][4 * i + q : 4 * i + q + 1, :], (META, BS))
                    hit = jnp.broadcast_to(tag.astype(jnp.bfloat16)[None], (8, META, BS)) > 0
                    picked = jnp.where(hit, blocks[u], picked)
                left[q % 2][i][q // 2] = picked.reshape(BS, BS)
        right = [
            jnp.concatenate([hbuf[r, pl.ds(j * BS, BS), :], hbuf[r, pl.ds((2 + j) * BS, BS), :]], axis=0)
            for j in range(2)
        ]
        for m in range(2):
            sums = []
            for j in range(2):
                rows = jnp.concatenate([jnp.concatenate(v, axis=1) for v in left[j][2 * m : 2 * m + 2]], axis=0)
                sums.append(jnp.dot(rows, right[j], preferred_element_type=jnp.float32))
            for j in range(2):
                acc[j, pl.ds(m * 2 * BS, 2 * BS), :] += sums[j]

    def multiply(reach, before):
        def one(r, carry):
            dz = jnp.int32(0)
            for c in (3 * r, 3 * r + 2):
                d = (sign * (c // 4 - z) + NZ + 6) % NZ - 6
                dz = jnp.maximum(dz, jnp.maximum(d, -d))
            d = (r // NYH - x + NX) % NX
            dx = jnp.minimum(d, NX - d)
            now = (dz <= reach[0]) & (dx <= reach[1])
            if before is not None:
                now = now & ((dz > before[0]) | (dx > before[1]))
            pl.when(now)(lambda: block_row(r))
            return carry

        lax.fori_loop(0, NX * NYH, one, 0)

    reached = None
    have = set()
    retired = 0
    for event in ORDER:
        kind, d = event[0], event[1]
        if kind == "C":
            multiply(event[1:], reached)
            reached = event[1:]
            continue
        here = receive(event)
        have.add(event if kind == "H" else (kind, d % 12))
        if kind in "EGA":
            low, high = (-5, 6) if kind == "A" else (-6, 5)
            if low < d <= 0:
                send("zp", here, (kind, d - 1))
            if 0 <= d < high:
                send("zm", here, (kind, d + 1))
        if kind == "E":
            send("y", here, ("B", d))
        if kind in "EG" and ("E", d % 12) in have and ("G", d % 12) in have:
            send("m", pbuf.at[col_of(d, False, False)], ("M", d))
        if kind in "AB" and ("A", d % 12) in have and ("B", d % 12) in have:
            send("m", pbuf.at[col_of(d, True, False)], ("N", d))
        if kind == "H":
            dy = event[2]
            if d == 0:
                if dy == -1:
                    send("hp", here, ("H", 0, -2))
                send("xp", here, ("H", -1, dy))
                send("xm", here, ("H", 1, dy))
            elif d == -1:
                send("xp", here, ("H", -2, dy))
        while retired < len(sent) - LAG:
            sent[retired].wait_send()
            retired += 1

    for i in range(4):
        for j in range(2):
            total = acc[j, pl.ds(i * BS, BS), :]
            kept = jnp.where(keep_ref[j, i] == 1, total, jnp.zeros_like(total))
            out_ref[i, j] = kept.astype(out_ref.dtype)
    for copy in sent[retired:]:
        copy.wait_send()


def shards(p_blocks, p_cols, h_blocks, h_rows, keep):
    hbm = pl.BlockSpec(memory_space=pltpu.HBM)
    return pl.pallas_call(
        kernel,
        out_shape=jax.ShapeDtypeStruct((4, 2, BS, BS), jnp.bfloat16),
        in_specs=[hbm] * 5,
        out_specs=pl.BlockSpec(memory_space=pltpu.VMEM),
        scratch_shapes=[
            pltpu.VMEM((NZ * 4, FULL, BS), jnp.bfloat16),
            pltpu.VMEM((NX * NYH, FULL, BS), jnp.bfloat16),
            pltpu.VMEM((2, ROWS, 2 * BS), jnp.bfloat16),
            pltpu.VMEM((2, ROWS, BS), jnp.float32),
            pltpu.SMEM((1, 4), jnp.int32),
            pltpu.SMEM((2, 2), jnp.int32),
            pltpu.SMEM((2, 4), jnp.int32),
            pltpu.SemaphoreType.DMA((96,)),
            pltpu.SemaphoreType.DMA((SEMS,)),
            pltpu.SemaphoreType.DMA((5,)),
        ],
        compiler_params=pltpu.CompilerParams(
            collective_id=0, has_side_effects=True, vmem_limit_bytes=60 * 1024 * 1024
        ),
        name="filtered_product",
    )(p_blocks.reshape(ROWS, BS), p_cols.reshape(1, 4), h_blocks.reshape(ROWS, BS), h_rows, keep.T)


def solution(mesh):
    return jax.shard_map(
        shards,
        mesh=mesh,
        in_specs=(
            P("row", "col", None, None),
            P("row", "col"),
            P("row", "col", None, None),
            P("row", "col"),
            P("row", "col"),
        ),
        out_specs=P("row", "col", None, None),
        check_vma=False,
    )
```

```python
import jax
import jax.numpy as jnp
from jax import lax
from jax.experimental import pallas as pl
from jax.experimental.pallas import tpu as pltpu
from jax.sharding import PartitionSpec as P

BS = 128
NX, NYH, NZ, NYL, NC = 4, 4, 12, 2, 2
ROWS = 4 * BS
META = 16
FULL = ROWS + META
SPLIT = 288
LAG = 41
MESH = pl.DeviceIdType.MESH

ORDER = [
    ("M", 0), ("E", -1), ("E", 1), ("A", 0), ("H", -1, 0), ("G", -1), ("G", 1), ("H", 1, 0), ("M", -1),
    ("E", -2), ("E", 2), ("M", 1), ("A", -1), ("H", 0, -1), ("H", -2, 0), ("A", 1), ("G", -2), ("G", 2),
    ("M", -2), ("E", -3), ("H", 0, 1), ("B", 0), ("E", 3), ("M", 2), ("H", -1, -1), ("A", -2), ("B", -1),
    ("N", 0), ("A", 2), ("H", 1, -1), ("G", -3), ("B", 1), ("N", -1), ("G", 3), ("H", -1, 1), ("M", -3),
    ("E", -4), ("B", -2), ("N", 1), ("E", 4), ("M", 3), ("H", 1, 1), ("B", 2), ("A", -3), ("N", -2), ("A", 3),
    ("H", -2, -1), ("N", 2), ("G", -4), ("G", 4), ("H", -2, 1), ("M", -4), ("E", -5), ("H", 0, -2), ("E", 5),
    ("M", 4), ("B", -3), ("A", -4), ("C", 2, 0), ("A", 4), ("B", 3), ("N", -3), ("G", -5), ("B", -4),
    ("G", 5), ("N", 3), ("H", -1, -2), ("E", -6), ("M", -5), ("B", 4), ("N", -4), ("A", -5), ("M", 5),
    ("H", 1, -2), ("A", 5), ("B", -5), ("N", 4), ("G", -6), ("C", 4, 1), ("B", 5), ("N", -5), ("H", -2, -2),
    ("M", -6), ("B", -6), ("A", 6), ("C", 4, 2), ("N", 5), ("C", 5, 2), ("N", 6), ("C", 6, 2),
]
FIRST = [
    ("y", ("A", 0)),
    ("zp", ("E", -1)),
    ("zm", ("E", 1)),
    ("zp", ("G", -1)),
    ("zm", ("G", 1)),
    ("hp", ("H", 0, -1)),
    ("hm", ("H", 0, 1)),
    ("xp", ("H", -1, 0)),
    ("xm", ("H", 1, 0)),
    ("y", ("B", 0)),
    ("m", ("M", 0)),
]
KINDS = {"E": 0, "A": 12, "B": 24, "M": 36, "N": 48, "G": 60}
SEMS = 88


def sem_index(event):
    if event[0] == "H":
        return 72 + (event[1] % 4) * 4 + event[2] % 4
    return KINDS[event[0]] + event[1] % 12


def kernel(
    p_ref, pc_hbm, h_ref, hr_hbm, keep_hbm, out_ref,
    pbuf, hbuf, lhs, acc, pc_ref, hr_ref, keep_ref, send_sem, recv_sem, own_sem,
):
    row, col = lax.axis_index("row"), lax.axis_index("col")
    x, yh = row // NYH, row % NYH
    z, yl, core = col // 4, (col // 2) % 2, col % 2
    sign = 1 - 2 * core

    def wrap(value, size):
        value = jnp.where(value < 0, value + size, value)
        return jnp.where(value >= size, value - size, value)

    z_base = {dz: wrap(z + sign * dz, NZ) * 4 for dz in range(-6, 6)}
    z_base[6] = z_base[-6]
    in_chip = {(p, c): (1 - yl if p else yl) * 2 + (1 - core if c else core) for p in (0, 1) for c in (0, 1)}
    x_base = {dx: wrap(x + sign * dx, NX) * NYH for dx in range(-2, 2)}
    y_at = {dy: wrap(yh + sign * dy, NYH) for dy in range(-2, 2)}

    def col_of(dz, flip_pair, flip_core):
        return z_base[dz] + in_chip[int(flip_pair), int(flip_core)]

    def row_of(dx, dy):
        return x_base[dx] + y_at[dy]

    links = {
        "zp": (row, col_of(1, False, False)),
        "zm": (row, col_of(-1, False, False)),
        "y": (row, col_of(0, True, False)),
        "m": (row, col_of(0, False, True)),
        "xp": (row_of(1, 0), col),
        "xm": (row_of(-1, 0), col),
        "hp": (row_of(0, 1), col),
        "hm": (row_of(0, -1), col),
    }
    head, tail = pl.ds(0, SPLIT), pl.ds(SPLIT, FULL - SPLIT)

    def region(event):
        kind, d = event[0], event[1]
        if kind == "H":
            return hbuf.at[row_of(d, event[2])]
        if kind == "E":
            return pbuf.at[col_of(d, False, False), tail]
        if kind == "G":
            return pbuf.at[col_of(d, False, False), head]
        if kind == "A":
            return pbuf.at[col_of(d, True, False), head]
        if kind == "B":
            return pbuf.at[col_of(d, True, False), tail]
        if kind == "M":
            return pbuf.at[col_of(-d, False, True)]
        return pbuf.at[col_of(-d, True, True)]

    barrier = pltpu.get_barrier_semaphore()
    for device in links.values():
        pl.semaphore_signal(barrier, inc=1, device_id=device, device_id_type=MESH)

    own = [
        pltpu.make_async_copy(pc_hbm, pc_ref, own_sem.at[0]),
        pltpu.make_async_copy(hr_hbm, hr_ref, own_sem.at[1]),
        pltpu.make_async_copy(keep_hbm, keep_ref, own_sem.at[2]),
        pltpu.make_async_copy(p_ref, pbuf.at[col, pl.ds(0, ROWS)], own_sem.at[3]),
        pltpu.make_async_copy(h_ref, hbuf.at[row, pl.ds(0, ROWS)], own_sem.at[4]),
    ]
    for copy in own:
        copy.start()
    acc[...] = jnp.zeros_like(acc)
    own[0].wait()
    own[1].wait()
    line = lax.broadcasted_iota(jnp.int32, (META, BS), 0)
    p_meta = jnp.zeros((META, BS), jnp.int32)
    h_meta = jnp.zeros((META, BS), jnp.int32)
    base = 48 * (col // 3)
    for i in range(4):
        value = pc_ref[0, i]
        p_meta = jnp.where(line // 4 == i, jnp.where(value < 0, -1, value - base), p_meta)
        value = hr_ref[i // 2, i % 2]
        h_meta = jnp.where(line % 4 == i, jnp.where(value < 0, -2, value - 48 * row), h_meta)
    pbuf[col, pl.ds(ROWS, META), :] = p_meta.astype(jnp.float32).astype(jnp.bfloat16)
    hbuf[row, pl.ds(ROWS, META), :] = h_meta.astype(jnp.float32).astype(jnp.bfloat16)
    for copy in own[2:]:
        copy.wait()
    pl.semaphore_wait(barrier, len(links))

    sent = []

    def send(link, source, event):
        copy = pltpu.make_async_remote_copy(
            src_ref=source,
            dst_ref=source,
            send_sem=send_sem.at[len(sent)],
            recv_sem=recv_sem.at[sem_index(event)],
            device_id=links[link],
            device_id_type=MESH,
        )
        copy.start()
        sent.append(copy)

    def receive(event):
        here = region(event)
        pltpu.make_async_remote_copy(
            src_ref=here,
            dst_ref=here,
            send_sem=send_sem.at[0],
            recv_sem=recv_sem.at[sem_index(event)],
            device_id=links["m"],
            device_id_type=MESH,
        ).wait_recv()
        return here

    own_part = {"A": pbuf.at[col, head], "G": pbuf.at[col, head], "B": pbuf.at[col, tail], "E": pbuf.at[col, tail]}
    own_part.update({"M": pbuf.at[col], "H": hbuf.at[row]})
    for link, event in FIRST:
        send(link, own_part[event[0]], event)

    def block_row(r):
        h_tags = hbuf[r, pl.ds(ROWS, META), :].astype(jnp.float32)
        tags = []
        for u in range(3):
            p_tags = pbuf[3 * r + u, pl.ds(ROWS, META), :].astype(jnp.float32)
            tags.append(jnp.where(p_tags == h_tags, 1.0, 0.0))
        left = [[[None, None] for _ in range(4)] for _ in range(2)]
        for i in range(4):
            blocks = [pbuf[3 * r + u, pl.ds(i * BS, BS), :].reshape(8, META, BS) for u in range(3)]
            for q in range(4):
                picked = jnp.zeros_like(blocks[0])
                for u in range(3):
                    tag = jnp.broadcast_to(tags[u][4 * i + q : 4 * i + q + 1, :], (META, BS))
                    hit = jnp.broadcast_to(tag.astype(jnp.bfloat16)[None], (8, META, BS)) > 0
                    picked = jnp.where(hit, blocks[u], picked)
                left[q % 2][i][q // 2] = picked.reshape(BS, BS)
        right = [
            jnp.concatenate([hbuf[r, pl.ds(j * BS, BS), :], hbuf[r, pl.ds((2 + j) * BS, BS), :]], axis=0)
            for j in range(2)
        ]
        for m in range(2):
            sums = []
            for j in range(2):
                rows = jnp.concatenate([jnp.concatenate(v, axis=1) for v in left[j][2 * m : 2 * m + 2]], axis=0)
                sums.append(jnp.dot(rows, right[j], preferred_element_type=jnp.float32))
            for j in range(2):
                acc[j, pl.ds(m * 2 * BS, 2 * BS), :] += sums[j]

    def edges(s):
        return (4 * (z + NZ - s) + 2) // 3, (4 * (z + NZ + s + 1)) // 3

    def multiply(reach, before):
        if before is not None and before[1] == reach[1] == 2:
            first, last = edges(reach[0]), edges(before[0])
            if reach[0] == 6:
                spans = [(last[1], last[0] + NX * NYH)]
            else:
                spans = [(first[0], last[0]), (last[1], first[1])]
            for span in spans:
                lax.fori_loop(span[0], span[1], lambda r, carry: block_row(r % (NX * NYH)) or carry, 0)
            return

        def one(r, carry):
            dz = jnp.int32(0)
            for c in (3 * r, 3 * r + 2):
                d = (sign * (c // 4 - z) + NZ + 6) % NZ - 6
                dz = jnp.maximum(dz, jnp.maximum(d, -d))
            d = (r // NYH - x + NX) % NX
            dx = jnp.minimum(d, NX - d)
            now = (dz <= reach[0]) & (dx <= reach[1])
            if before is not None:
                now = now & ((dz > before[0]) | (dx > before[1]))
            pl.when(now)(lambda: block_row(r))
            return carry

        lax.fori_loop(0, NX * NYH, one, 0)

    reached = None
    have = set()
    retired = 0
    for event in ORDER:
        kind, d = event[0], event[1]
        if kind == "C":
            multiply(event[1:], reached)
            reached = event[1:]
            continue
        here = receive(event)
        have.add(event if kind == "H" else (kind, d % 12))
        if kind in "EGA":
            low, high = (-5, 6) if kind == "A" else (-6, 5)
            if low < d <= 0:
                send("zp", here, (kind, d - 1))
            if 0 <= d < high:
                send("zm", here, (kind, d + 1))
        if kind == "E":
            send("y", here, ("B", d))
        if kind in "EG" and ("E", d % 12) in have and ("G", d % 12) in have:
            send("m", pbuf.at[col_of(d, False, False)], ("M", d))
        if kind in "AB" and ("A", d % 12) in have and ("B", d % 12) in have:
            send("m", pbuf.at[col_of(d, True, False)], ("N", d))
        if kind == "H":
            dy = event[2]
            if d == 0:
                if dy == -1:
                    send("hp", here, ("H", 0, -2))
                send("xp", here, ("H", -1, dy))
                send("xm", here, ("H", 1, dy))
            elif d == -1:
                send("xp", here, ("H", -2, dy))
        while retired < len(sent) - LAG:
            sent[retired].wait_send()
            retired += 1

    for i in range(4):
        for j in range(2):
            total = acc[j, pl.ds(i * BS, BS), :]
            kept = jnp.where(keep_ref[j, i] == 1, total, jnp.zeros_like(total))
            out_ref[i, j] = kept.astype(out_ref.dtype)
    for copy in sent[retired:]:
        copy.wait_send()


def shards(p_blocks, p_cols, h_blocks, h_rows, keep):
    hbm = pl.BlockSpec(memory_space=pltpu.HBM)
    return pl.pallas_call(
        kernel,
        out_shape=jax.ShapeDtypeStruct((4, 2, BS, BS), jnp.bfloat16),
        in_specs=[hbm] * 5,
        out_specs=pl.BlockSpec(memory_space=pltpu.VMEM),
        scratch_shapes=[
            pltpu.VMEM((NZ * 4, FULL, BS), jnp.bfloat16),
            pltpu.VMEM((NX * NYH, FULL, BS), jnp.bfloat16),
            pltpu.VMEM((2, ROWS, 2 * BS), jnp.bfloat16),
            pltpu.VMEM((2, ROWS, BS), jnp.float32),
            pltpu.SMEM((1, 4), jnp.int32),
            pltpu.SMEM((2, 2), jnp.int32),
            pltpu.SMEM((2, 4), jnp.int32),
            pltpu.SemaphoreType.DMA((96,)),
            pltpu.SemaphoreType.DMA((SEMS,)),
            pltpu.SemaphoreType.DMA((5,)),
        ],
        compiler_params=pltpu.CompilerParams(
            collective_id=0, has_side_effects=True, vmem_limit_bytes=24 * 1024 * 1024
        ),
        name="filtered_product",
    )(*[
        pltpu.with_memory_space_constraint(array, pltpu.HBM)
        for array in (p_blocks.reshape(ROWS, BS), p_cols.reshape(1, 4), h_blocks.reshape(ROWS, BS), h_rows, keep.T)
    ])


def solution(mesh):
    return jax.shard_map(
        shards,
        mesh=mesh,
        in_specs=(
            P("row", "col", None, None),
            P("row", "col"),
            P("row", "col", None, None),
            P("row", "col"),
            P("row", "col"),
        ),
        out_specs=P("row", "col", None, None),
        check_vma=False,
    )
```

```python
import jax
import jax.numpy as jnp
from jax import lax
from jax.experimental import pallas as pl
from jax.experimental.pallas import tpu as pltpu
from jax.sharding import PartitionSpec as P

BS = 128
NX, NYH, NZ, NYL, NC = 4, 4, 12, 2, 2
ROWS = 4 * BS
META = 16
FULL = ROWS + META
SPLIT = 288
NEAR = 6
LAG = 41
LAST_LAG = 12
MESH = pl.DeviceIdType.MESH

ORDER = [
    ("M", 0), ("E", -1), ("E", 1), ("A", 0), ("H", -1, 0), ("G", -1), ("G", 1), ("H", 1, 0), ("M", -1),
    ("E", -2), ("E", 2), ("M", 1), ("A", -1), ("H", 0, -1), ("H", -2, 0), ("A", 1), ("G", -2), ("G", 2),
    ("M", -2), ("E", -3), ("H", 0, 1), ("B", 0), ("E", 3), ("M", 2), ("H", -1, -1), ("A", -2), ("B", -1),
    ("N", 0), ("A", 2), ("H", 1, -1), ("G", -3), ("B", 1), ("N", -1), ("G", 3), ("H", -1, 1), ("M", -3),
    ("E", -4), ("B", -2), ("N", 1), ("E", 4), ("M", 3), ("H", 1, 1), ("B", 2), ("A", -3), ("N", -2), ("A", 3),
    ("H", -2, -1), ("N", 2), ("G", -4), ("G", 4), ("H", -2, 1), ("M", -4), ("E", -5), ("H", 0, -2), ("E", 5),
    ("M", 4), ("B", -3), ("A", -4), ("C", 2, 0), ("A", 4), ("B", 3), ("N", -3), ("G", -5), ("B", -4),
    ("G", 5), ("N", 3), ("H", -1, -2), ("E", -6), ("M", -5), ("B", 4), ("N", -4), ("A", -5), ("M", 5),
    ("H", 1, -2), ("A", 5), ("B", -5), ("N", 4), ("G", -6), ("C", 4, 1), ("B", 5), ("N", -5), ("H", -2, -2),
    ("M", -6), ("B", -6), ("A", 6), ("C", 4, 2), ("N", 5), ("C", 5, 2), ("N", 6), ("C", 6, 2),
]
FIRST = [
    ("y", ("A", 0)),
    ("zp", ("E", -1)),
    ("zm", ("E", 1)),
    ("zp", ("G", -1)),
    ("zm", ("G", 1)),
    ("hp", ("H", 0, -1)),
    ("hm", ("H", 0, 1)),
    ("xp", ("H", -1, 0)),
    ("xm", ("H", 1, 0)),
    ("y", ("B", 0)),
    ("m", ("M", 0)),
]
KINDS = {"E": 0, "A": 12, "B": 24, "M": 36, "N": 48, "G": 60}
SEMS = 88


def sem_index(event):
    if event[0] == "H":
        return 72 + (event[1] % 4) * 4 + event[2] % 4
    return KINDS[event[0]] + event[1] % 12


def kernel(
    p_ref, pc_hbm, h_ref, hr_hbm, keep_hbm, out_ref,
    pbuf, hbuf, lhs, acc, pc_ref, hr_ref, keep_ref, send_sem, recv_sem, own_sem,
):
    row, col = lax.axis_index("row"), lax.axis_index("col")
    x, yh = row // NYH, row % NYH
    z, yl, core = col // 4, (col // 2) % 2, col % 2
    sign = 1 - 2 * core

    def wrap(value, size):
        value = jnp.where(value < 0, value + size, value)
        return jnp.where(value >= size, value - size, value)

    z_base = {dz: wrap(z + sign * dz, NZ) * 4 for dz in range(-6, 6)}
    z_base[6] = z_base[-6]
    in_chip = {(p, c): (1 - yl if p else yl) * 2 + (1 - core if c else core) for p in (0, 1) for c in (0, 1)}
    x_base = {dx: wrap(x + sign * dx, NX) * NYH for dx in range(-2, 2)}
    y_at = {dy: wrap(yh + sign * dy, NYH) for dy in range(-2, 2)}

    def col_of(dz, flip_pair, flip_core):
        return z_base[dz] + in_chip[int(flip_pair), int(flip_core)]

    def row_of(dx, dy):
        return x_base[dx] + y_at[dy]

    links = {
        "zp": (row, col_of(1, False, False)),
        "zm": (row, col_of(-1, False, False)),
        "y": (row, col_of(0, True, False)),
        "m": (row, col_of(0, False, True)),
        "xp": (row_of(1, 0), col),
        "xm": (row_of(-1, 0), col),
        "hp": (row_of(0, 1), col),
        "hm": (row_of(0, -1), col),
    }
    head, tail = pl.ds(0, SPLIT), pl.ds(SPLIT, FULL - SPLIT)

    def region(event):
        kind, d = event[0], event[1]
        if kind == "H":
            return hbuf.at[row_of(d, event[2])]
        if kind == "E":
            return pbuf.at[col_of(d, False, False), tail]
        if kind == "G":
            return pbuf.at[col_of(d, False, False), head]
        if kind == "A":
            return pbuf.at[col_of(d, True, False), head]
        if kind == "B":
            return pbuf.at[col_of(d, True, False), tail]
        if kind == "M":
            return pbuf.at[col_of(-d, False, True)]
        return pbuf.at[col_of(-d, True, True)]

    barrier = pltpu.get_barrier_semaphore()
    for device in links.values():
        pl.semaphore_signal(barrier, inc=1, device_id=device, device_id_type=MESH)

    own = [
        pltpu.make_async_copy(pc_hbm, pc_ref, own_sem.at[0]),
        pltpu.make_async_copy(hr_hbm, hr_ref, own_sem.at[1]),
        pltpu.make_async_copy(keep_hbm, keep_ref, own_sem.at[2]),
        pltpu.make_async_copy(p_ref, pbuf.at[col, pl.ds(META, ROWS)], own_sem.at[3]),
        pltpu.make_async_copy(h_ref, hbuf.at[row, pl.ds(META, ROWS)], own_sem.at[4]),
    ]
    for copy in own:
        copy.start()
    sent = []

    def send(link, source, event):
        copy = pltpu.make_async_remote_copy(
            src_ref=source,
            dst_ref=region(("E", 0)) if event in (("E", 1), ("E", -1)) else source,
            send_sem=send_sem.at[len(sent)],
            recv_sem=recv_sem.at[sem_index(event)],
            device_id=links[link],
            device_id_type=MESH,
        )
        copy.start()
        sent.append(copy)

    def receive(event):
        here = region(event)
        pltpu.make_async_remote_copy(
            src_ref=here,
            dst_ref=here,
            send_sem=send_sem.at[0],
            recv_sem=recv_sem.at[sem_index(event)],
            device_id=links["m"],
            device_id_type=MESH,
        ).wait_recv()
        return here

    pl.semaphore_wait(barrier, len(links))
    rest = p_ref.at[pl.ds(SPLIT - META, FULL - SPLIT)]
    send("zp", rest, ("E", -1))
    send("zm", rest, ("E", 1))
    acc[...] = jnp.zeros_like(acc)
    own[0].wait()
    own[1].wait()
    line = lax.broadcasted_iota(jnp.int32, (META, BS), 0)
    p_meta = jnp.zeros((META, BS), jnp.int32)
    h_meta = jnp.zeros((META, BS), jnp.int32)
    base = 48 * (col // 3)
    for i in range(4):
        value = pc_ref[0, i]
        p_meta = jnp.where(line // 4 == i, jnp.where(value < 0, -1, value - base), p_meta)
        value = hr_ref[i // 2, i % 2]
        h_meta = jnp.where(line % 4 == i, jnp.where(value < 0, -2, value - 48 * row), h_meta)
    pbuf[col, pl.ds(0, META), :] = p_meta.astype(jnp.float32).astype(jnp.bfloat16)
    hbuf[row, pl.ds(0, META), :] = h_meta.astype(jnp.float32).astype(jnp.bfloat16)
    for copy in own[2:]:
        copy.wait()
    own_part = {"A": pbuf.at[col, head], "G": pbuf.at[col, head], "B": pbuf.at[col, tail]}
    own_part.update({"M": pbuf.at[col], "H": hbuf.at[row]})
    for link, event in FIRST:
        if event[0] != "E":
            send(link, own_part[event[0]], event)

    def block_row(r):
        h_tags = hbuf[r, pl.ds(0, META), :].astype(jnp.float32)
        tags = []
        for u in range(3):
            p_tags = pbuf[3 * r + u, pl.ds(0, META), :].astype(jnp.float32)
            tags.append(jnp.where(p_tags == h_tags, 1.0, 0.0))
        left = [[[None, None] for _ in range(4)] for _ in range(2)]
        for i in range(4):
            blocks = [pbuf[3 * r + u, pl.ds(META + i * BS, BS), :].reshape(8, META, BS) for u in range(3)]
            for q in range(4):
                picked = jnp.zeros_like(blocks[0])
                for u in range(3):
                    tag = jnp.broadcast_to(tags[u][4 * i + q : 4 * i + q + 1, :], (META, BS))
                    hit = jnp.broadcast_to(tag.astype(jnp.bfloat16)[None], (8, META, BS)) > 0
                    picked = jnp.where(hit, blocks[u], picked)
                left[q % 2][i][q // 2] = picked.reshape(BS, BS)
        right = [
            jnp.concatenate([hbuf[r, pl.ds(META + j * BS, BS), :], hbuf[r, pl.ds(META + (2 + j) * BS, BS), :]], axis=0)
            for j in range(2)
        ]
        for m in range(2):
            sums = []
            for j in range(2):
                rows = jnp.concatenate([jnp.concatenate(v, axis=1) for v in left[j][2 * m : 2 * m + 2]], axis=0)
                sums.append(jnp.dot(rows, right[j], preferred_element_type=jnp.float32))
            for j in range(2):
                acc[j, pl.ds(m * 2 * BS, 2 * BS), :] += sums[j]

    def edges(s):
        return (4 * (z + NZ - s) + 2) // 3, (4 * (z + NZ + s + 1)) // 3

    def multiply(reach, before):
        if before is not None and before[1] == reach[1] == 2:
            first, last = edges(reach[0]), edges(before[0])
            if reach[0] == 6:
                spans = [(last[1], last[0] + NX * NYH)]
            else:
                spans = [(first[0], last[0]), (last[1], first[1])]
            for span in spans:
                lax.fori_loop(span[0], span[1], lambda r, carry: block_row(r % (NX * NYH)) or carry, 0)
            return

        def one(r, carry):
            dz = jnp.int32(0)
            for c in (3 * r, 3 * r + 2):
                d = (sign * (c // 4 - z) + NZ + 6) % NZ - 6
                dz = jnp.maximum(dz, jnp.maximum(d, -d))
            d = (r // NYH - x + NX) % NX
            dx = jnp.minimum(d, NX - d)
            now = (dz <= reach[0]) & (dx <= reach[1])
            if before is not None:
                now = now & ((dz > before[0]) | (dx > before[1]))
            pl.when(now)(lambda: block_row(r))
            return carry

        lax.fori_loop(0, NX * NYH, one, 0)

    reached = None
    have = set()
    retired = 0
    for place, event in enumerate(ORDER):
        kind, d = event[0], event[1]
        if kind == "C":
            multiply(event[1:], reached)
            reached = event[1:]
            continue
        here = receive(event)
        have.add(event if kind == "H" else (kind, d % 12))
        if kind in "EGA":
            low, high = (-5, 6) if kind == "A" else (-6, 5)
            if low < d <= 0:
                send("zp", here, (kind, d - 1))
            if 0 <= d < high:
                send("zm", here, (kind, d + 1))
        if kind == "E" and abs(d) <= NEAR:
            send("y", here, ("B", d))
        if kind == "B" and -5 < d <= -NEAR:
            send("zp", here, ("B", d - 1))
        if kind == "B" and NEAR <= d < 6:
            send("zm", here, ("B", d + 1))
        if kind in "EG" and ("E", d % 12) in have and ("G", d % 12) in have:
            send("m", pbuf.at[col_of(d, False, False)], ("M", d))
        if kind in "AB" and ("A", d % 12) in have and ("B", d % 12) in have:
            send("m", pbuf.at[col_of(d, True, False)], ("N", d))
        if kind == "H":
            dy = event[2]
            if d == 0:
                if dy == -1:
                    send("hp", here, ("H", 0, -2))
                send("xp", here, ("H", -1, dy))
                send("xm", here, ("H", 1, dy))
            elif d == -1:
                send("xp", here, ("H", -2, dy))
        lag = LAG if place < len(ORDER) - 8 else LAST_LAG
        while retired < len(sent) - lag:
            sent[retired].wait_send()
            retired += 1

    for i in range(4):
        for j in range(2):
            total = acc[j, pl.ds(i * BS, BS), :]
            kept = jnp.where(keep_ref[j, i] == 1, total, jnp.zeros_like(total))
            out_ref[i, j] = kept.astype(out_ref.dtype)
    for copy in sent[retired:]:
        copy.wait_send()


def shards(p_blocks, p_cols, h_blocks, h_rows, keep):
    hbm = pl.BlockSpec(memory_space=pltpu.HBM)
    return pl.pallas_call(
        kernel,
        out_shape=jax.ShapeDtypeStruct((4, 2, BS, BS), jnp.bfloat16),
        in_specs=[hbm] * 5,
        out_specs=pl.BlockSpec(memory_space=pltpu.VMEM),
        scratch_shapes=[
            pltpu.VMEM((NZ * 4, FULL, BS), jnp.bfloat16),
            pltpu.VMEM((NX * NYH, FULL, BS), jnp.bfloat16),
            pltpu.VMEM((2, ROWS, 2 * BS), jnp.bfloat16),
            pltpu.VMEM((2, ROWS, BS), jnp.float32),
            pltpu.SMEM((1, 4), jnp.int32),
            pltpu.SMEM((2, 2), jnp.int32),
            pltpu.SMEM((2, 4), jnp.int32),
            pltpu.SemaphoreType.DMA((96,)),
            pltpu.SemaphoreType.DMA((SEMS,)),
            pltpu.SemaphoreType.DMA((5,)),
        ],
        compiler_params=pltpu.CompilerParams(
            collective_id=0, has_side_effects=True, vmem_limit_bytes=24 * 1024 * 1024
        ),
        name="filtered_product",
    )(*[
        pltpu.with_memory_space_constraint(array, pltpu.HBM)
        for array in (p_blocks.reshape(ROWS, BS), p_cols.reshape(1, 4), h_blocks.reshape(ROWS, BS), h_rows, keep.T)
    ])


def solution(mesh):
    return jax.shard_map(
        shards,
        mesh=mesh,
        in_specs=(
            P("row", "col", None, None),
            P("row", "col"),
            P("row", "col", None, None),
            P("row", "col"),
            P("row", "col"),
        ),
        out_specs=P("row", "col", None, None),
        check_vma=False,
    )
```

```python
import jax
import jax.numpy as jnp
from jax import lax
from jax.experimental import pallas as pl
from jax.experimental.pallas import tpu as pltpu
from jax.sharding import PartitionSpec as P

BS = 128
NX, NYH, NZ, NYL, NC = 4, 4, 12, 2, 2
ROWS = 4 * BS
META = 16
FULL = ROWS + META
SPLIT = 256
LAG = 42
MESH = pl.DeviceIdType.MESH

ORDER = [
    ("M", 0), ("E", -1), ("A", 0), ("E", 1), ("H", -1, 0), ("G", -1), ("G", 1), ("H", 1, 0), ("M", -1),
    ("E", -2), ("M", 1), ("A", -1), ("H", 0, -1), ("A", 1), ("H", -2, 0), ("E", 2), ("G", -2), ("G", 2),
    ("H", 0, 1), ("M", -2), ("E", -3), ("B", 0), ("M", 2), ("A", -2), ("H", -1, -1), ("A", 2), ("N", 0),
    ("B", -1), ("E", 3), ("H", 1, -1), ("G", -3), ("N", -1), ("G", 3), ("B", 1), ("H", -1, 1), ("M", -3),
    ("E", -4), ("A", -3), ("M", 3), ("H", 1, 1), ("B", -2), ("N", 1), ("A", 3), ("E", 4), ("H", -2, -1),
    ("N", -2), ("G", -4), ("G", 4), ("H", -2, 1), ("M", -4), ("E", -5), ("H", 0, -2), ("M", 4), ("A", -4),
    ("B", 2), ("A", 4), ("C", 1, 0), ("E", 5), ("N", 2), ("B", -3), ("G", -5), ("C", 2, 0), ("G", 5),
    ("B", 3), ("N", -3), ("H", -1, -2), ("M", -5), ("E", -6), ("A", -5), ("M", 5), ("N", 3), ("B", -4),
    ("H", 1, -2), ("A", 5), ("C", 3, 1), ("G", -6), ("N", -4), ("B", 4), ("H", -2, -2), ("B", -5), ("A", 6),
    ("C", 3, 2), ("M", -6), ("B", 5), ("N", 4), ("N", -5), ("C", 4, 2), ("B", -6), ("N", 5), ("C", 5, 2),
    ("N", -6), ("C", 6, 2),
]
FIRST = [
    ("y", ("A", 0)),
    ("zp", ("E", -1)),
    ("zm", ("E", 1)),
    ("zp", ("G", -1)),
    ("zm", ("G", 1)),
    ("hp", ("H", 0, -1)),
    ("hm", ("H", 0, 1)),
    ("xp", ("H", -1, 0)),
    ("xm", ("H", 1, 0)),
    ("y", ("B", 0)),
    ("m", ("M", 0)),
]
KINDS = {"E": 0, "A": 12, "B": 24, "M": 36, "N": 48, "G": 60}
SEMS = 88


def sem_index(event):
    if event[0] == "H":
        return 72 + (event[1] % 4) * 4 + event[2] % 4
    return KINDS[event[0]] + event[1] % 12


def kernel(
    p_ref, pc_hbm, h_ref, hr_hbm, keep_hbm, out_ref,
    pbuf, hbuf, lhs, acc, pc_ref, hr_ref, keep_ref, send_sem, recv_sem, own_sem,
):
    row, col = lax.axis_index("row"), lax.axis_index("col")
    x, yh = row // NYH, row % NYH
    z, yl, core = col // 4, (col // 2) % 2, col % 2
    sign = 1 - 2 * core

    def wrap(value, size):
        value = jnp.where(value < 0, value + size, value)
        return jnp.where(value >= size, value - size, value)

    z_base = {dz: wrap(z + sign * dz, NZ) * 4 for dz in range(-6, 6)}
    z_base[6] = z_base[-6]
    in_chip = {(p, c): (1 - yl if p else yl) * 2 + (1 - core if c else core) for p in (0, 1) for c in (0, 1)}
    x_base = {dx: wrap(x + sign * dx, NX) * NYH for dx in range(-2, 2)}
    y_at = {dy: wrap(yh + sign * dy, NYH) for dy in range(-2, 2)}

    def col_of(dz, flip_pair, flip_core):
        return z_base[dz] + in_chip[int(flip_pair), int(flip_core)]

    def row_of(dx, dy):
        return x_base[dx] + y_at[dy]

    links = {
        "zp": (row, col_of(1, False, False)),
        "zm": (row, col_of(-1, False, False)),
        "y": (row, col_of(0, True, False)),
        "m": (row, col_of(0, False, True)),
        "xp": (row_of(1, 0), col),
        "xm": (row_of(-1, 0), col),
        "hp": (row_of(0, 1), col),
        "hm": (row_of(0, -1), col),
    }
    head, tail = pl.ds(0, SPLIT), pl.ds(SPLIT, FULL - SPLIT)

    def region(event):
        kind, d = event[0], event[1]
        if kind == "H":
            return hbuf.at[row_of(d, event[2])]
        if kind == "E":
            return pbuf.at[col_of(d, False, False), tail]
        if kind == "G":
            return pbuf.at[col_of(d, False, False), head]
        if kind == "A":
            return pbuf.at[col_of(d, True, False), head]
        if kind == "B":
            return pbuf.at[col_of(d, True, False), tail]
        if kind == "M":
            return pbuf.at[col_of(-d, False, True)]
        return pbuf.at[col_of(-d, True, True)]

    barrier = pltpu.get_barrier_semaphore()
    for device in links.values():
        pl.semaphore_signal(barrier, inc=1, device_id=device, device_id_type=MESH)

    own = [
        pltpu.make_async_copy(pc_hbm, pc_ref, own_sem.at[0]),
        pltpu.make_async_copy(hr_hbm, hr_ref, own_sem.at[1]),
        pltpu.make_async_copy(keep_hbm, keep_ref, own_sem.at[2]),
        pltpu.make_async_copy(p_ref, pbuf.at[col, pl.ds(0, ROWS)], own_sem.at[3]),
        pltpu.make_async_copy(h_ref, hbuf.at[row, pl.ds(0, ROWS)], own_sem.at[4]),
    ]
    for copy in own:
        copy.start()
    acc[...] = jnp.zeros_like(acc)
    own[0].wait()
    own[1].wait()
    line = lax.broadcasted_iota(jnp.int32, (META, BS), 0)
    p_meta = jnp.zeros((META, BS), jnp.int32)
    h_meta = jnp.zeros((META, BS), jnp.int32)
    base = 48 * (col // 3)
    for i in range(4):
        value = pc_ref[0, i]
        p_meta = jnp.where(line // 4 == i, jnp.where(value < 0, -1, value - base), p_meta)
        value = hr_ref[i // 2, i % 2]
        h_meta = jnp.where(line % 4 == i, jnp.where(value < 0, -2, value - 48 * row), h_meta)
    pbuf[col, pl.ds(ROWS, META), :] = p_meta.astype(jnp.float32).astype(jnp.bfloat16)
    hbuf[row, pl.ds(ROWS, META), :] = h_meta.astype(jnp.float32).astype(jnp.bfloat16)
    for copy in own[2:]:
        copy.wait()
    pl.semaphore_wait(barrier, len(links))

    sent = []

    def send(link, source, event):
        copy = pltpu.make_async_remote_copy(
            src_ref=source,
            dst_ref=source,
            send_sem=send_sem.at[len(sent)],
            recv_sem=recv_sem.at[sem_index(event)],
            device_id=links[link],
            device_id_type=MESH,
        )
        copy.start()
        sent.append(copy)

    def receive(event):
        here = region(event)
        pltpu.make_async_remote_copy(
            src_ref=here,
            dst_ref=here,
            send_sem=send_sem.at[0],
            recv_sem=recv_sem.at[sem_index(event)],
            device_id=links["m"],
            device_id_type=MESH,
        ).wait_recv()
        return here

    own_part = {"A": pbuf.at[col, head], "G": pbuf.at[col, head], "B": pbuf.at[col, tail], "E": pbuf.at[col, tail]}
    own_part.update({"M": pbuf.at[col], "H": hbuf.at[row]})
    for link, event in FIRST:
        send(link, own_part[event[0]], event)

    def block_row(r):
        h_tags = hbuf[r, pl.ds(ROWS, META), :].astype(jnp.float32)
        tags = []
        for u in range(3):
            p_tags = pbuf[3 * r + u, pl.ds(ROWS, META), :].astype(jnp.float32)
            tags.append(jnp.where(p_tags == h_tags, 1.0, 0.0))
        left = [[[None, None] for _ in range(4)] for _ in range(2)]
        for i in range(4):
            blocks = [pbuf[3 * r + u, pl.ds(i * BS, BS), :].reshape(8, META, BS) for u in range(3)]
            for q in range(4):
                picked = jnp.zeros_like(blocks[0])
                for u in range(3):
                    tag = jnp.broadcast_to(tags[u][4 * i + q : 4 * i + q + 1, :], (META, BS))
                    hit = jnp.broadcast_to(tag.astype(jnp.bfloat16)[None], (8, META, BS)) > 0
                    picked = jnp.where(hit, blocks[u], picked)
                left[q % 2][i][q // 2] = picked.reshape(BS, BS)
        right = [
            jnp.concatenate([hbuf[r, pl.ds(j * BS, BS), :], hbuf[r, pl.ds((2 + j) * BS, BS), :]], axis=0)
            for j in range(2)
        ]
        for m in range(2):
            sums = []
            for j in range(2):
                rows = jnp.concatenate([jnp.concatenate(v, axis=1) for v in left[j][2 * m : 2 * m + 2]], axis=0)
                sums.append(jnp.dot(rows, right[j], preferred_element_type=jnp.float32))
            for j in range(2):
                acc[j, pl.ds(m * 2 * BS, 2 * BS), :] += sums[j]

    def edges(s):
        return (4 * (z + NZ - s) + 2) // 3, (4 * (z + NZ + s + 1)) // 3

    def multiply(reach, before):
        if before is not None and before[1] == reach[1] == 2:
            first, last = edges(reach[0]), edges(before[0])
            if reach[0] == 6:
                spans = [(last[1], last[0] + NX * NYH)]
            else:
                spans = [(first[0], last[0]), (last[1], first[1])]
            for span in spans:
                lax.fori_loop(span[0], span[1], lambda r, carry: block_row(r % (NX * NYH)) or carry, 0)
            return

        def one(r, carry):
            dz = jnp.int32(0)
            for c in (3 * r, 3 * r + 2):
                d = (sign * (c // 4 - z) + NZ + 6) % NZ - 6
                dz = jnp.maximum(dz, jnp.maximum(d, -d))
            d = (r // NYH - x + NX) % NX
            dx = jnp.minimum(d, NX - d)
            now = (dz <= reach[0]) & (dx <= reach[1])
            if before is not None:
                now = now & ((dz > before[0]) | (dx > before[1]))
            pl.when(now)(lambda: block_row(r))
            return carry

        lax.fori_loop(0, NX * NYH, one, 0)

    reached = None
    have = set()
    retired = 0
    for event in ORDER:
        kind, d = event[0], event[1]
        if kind == "C":
            multiply(event[1:], reached)
            reached = event[1:]
            continue
        here = receive(event)
        have.add(event if kind == "H" else (kind, d % 12))
        if kind in "EGA":
            low, high = (-5, 6) if kind == "A" else (-6, 5)
            if low < d <= 0:
                send("zp", here, (kind, d - 1))
            if 0 <= d < high:
                send("zm", here, (kind, d + 1))
        if kind == "E":
            send("y", here, ("B", d))
        if kind in "EG" and ("E", d % 12) in have and ("G", d % 12) in have:
            send("m", pbuf.at[col_of(d, False, False)], ("M", d))
        if kind in "AB" and ("A", d % 12) in have and ("B", d % 12) in have:
            send("m", pbuf.at[col_of(d, True, False)], ("N", d))
        if kind == "H":
            dy = event[2]
            if d == 0:
                if dy == -1:
                    send("hp", here, ("H", 0, -2))
                send("xp", here, ("H", -1, dy))
                send("xm", here, ("H", 1, dy))
            elif d == -1:
                send("xp", here, ("H", -2, dy))
        while retired < len(sent) - LAG:
            sent[retired].wait_send()
            retired += 1

    for i in range(4):
        for j in range(2):
            total = acc[j, pl.ds(i * BS, BS), :]
            kept = jnp.where(keep_ref[j, i] == 1, total, jnp.zeros_like(total))
            out_ref[i, j] = kept.astype(out_ref.dtype)
    for copy in sent[retired:]:
        copy.wait_send()


def shards(p_blocks, p_cols, h_blocks, h_rows, keep):
    hbm = pl.BlockSpec(memory_space=pltpu.HBM)
    return pl.pallas_call(
        kernel,
        out_shape=jax.ShapeDtypeStruct((4, 2, BS, BS), jnp.bfloat16),
        in_specs=[hbm] * 5,
        out_specs=pl.BlockSpec(memory_space=pltpu.VMEM),
        scratch_shapes=[
            pltpu.VMEM((NZ * 4, FULL, BS), jnp.bfloat16),
            pltpu.VMEM((NX * NYH, FULL, BS), jnp.bfloat16),
            pltpu.VMEM((2, ROWS, 2 * BS), jnp.bfloat16),
            pltpu.VMEM((2, ROWS, BS), jnp.float32),
            pltpu.SMEM((1, 4), jnp.int32),
            pltpu.SMEM((2, 2), jnp.int32),
            pltpu.SMEM((2, 4), jnp.int32),
            pltpu.SemaphoreType.DMA((96,)),
            pltpu.SemaphoreType.DMA((SEMS,)),
            pltpu.SemaphoreType.DMA((5,)),
        ],
        compiler_params=pltpu.CompilerParams(
            collective_id=0, has_side_effects=True, vmem_limit_bytes=24 * 1024 * 1024
        ),
        name="filtered_product",
    )(*[
        pltpu.with_memory_space_constraint(array, pltpu.HBM)
        for array in (p_blocks.reshape(ROWS, BS), p_cols.reshape(1, 4), h_blocks.reshape(ROWS, BS), h_rows, keep.T)
    ])


def solution(mesh):
    return jax.shard_map(
        shards,
        mesh=mesh,
        in_specs=(
            P("row", "col", None, None),
            P("row", "col"),
            P("row", "col", None, None),
            P("row", "col"),
            P("row", "col"),
        ),
        out_specs=P("row", "col", None, None),
        check_vma=False,
    )
```

```python
import jax
import jax.numpy as jnp
from jax import lax
from jax.experimental import pallas as pl
from jax.experimental.pallas import tpu as pltpu
from jax.sharding import PartitionSpec as P

BS = 128
NX, NYH, NZ, NYL, NC = 4, 4, 12, 2, 2
ROWS = 4 * BS
META = 16
FULL = ROWS + META
SPLIT = 256
LAG = 42
MESH = pl.DeviceIdType.MESH

ORDER = [
    ("M", 0), ("E", -1), ("A", 0), ("E", 1), ("H", -1, 0), ("G", -1), ("G", 1), ("H", 1, 0), ("M", -1),
    ("E", -2), ("M", 1), ("A", -1), ("H", 0, -1), ("A", 1), ("H", -2, 0), ("E", 2), ("G", -2), ("G", 2),
    ("H", 0, 1), ("M", -2), ("E", -3), ("B", 0), ("M", 2), ("A", -2), ("H", -1, -1), ("A", 2), ("N", 0),
    ("B", -1), ("E", 3), ("H", 1, -1), ("G", -3), ("N", -1), ("G", 3), ("B", 1), ("H", -1, 1), ("M", -3),
    ("E", -4), ("A", -3), ("M", 3), ("H", 1, 1), ("B", -2), ("N", 1), ("A", 3), ("E", 4), ("H", -2, -1),
    ("N", -2), ("G", -4), ("G", 4), ("H", -2, 1), ("M", -4), ("E", -5), ("H", 0, -2), ("M", 4), ("A", -4),
    ("B", 2), ("A", 4), ("E", 5), ("N", 2), ("B", -3), ("G", -5), ("C", 2, 0), ("G", 5),
    ("B", 3), ("N", -3), ("H", -1, -2), ("M", -5), ("E", -6), ("A", -5), ("M", 5), ("N", 3), ("B", -4),
    ("H", 1, -2), ("A", 5), ("C", 3, 1), ("G", -6), ("N", -4), ("B", 4), ("H", -2, -2), ("B", -5), ("A", 6),
    ("C", 3, 2), ("M", -6), ("B", 5), ("N", 4), ("N", -5), ("C", 4, 2), ("B", -6), ("N", 5), ("C", 5, 2),
    ("N", -6), ("C", 6, 2),
]
FIRST = [
    ("y", ("A", 0)),
    ("zp", ("E", -1)),
    ("zm", ("E", 1)),
    ("zp", ("G", -1)),
    ("zm", ("G", 1)),
    ("hp", ("H", 0, -1)),
    ("hm", ("H", 0, 1)),
    ("xp", ("H", -1, 0)),
    ("xm", ("H", 1, 0)),
    ("y", ("B", 0)),
    ("m", ("M", 0)),
]
KINDS = {"E": 0, "A": 12, "B": 24, "M": 36, "N": 48, "G": 60}
SEMS = 88


def sem_index(event):
    if event[0] == "H":
        return 72 + (event[1] % 4) * 4 + event[2] % 4
    return KINDS[event[0]] + event[1] % 12


def kernel(
    p_ref, pc_hbm, h_ref, hr_hbm, keep_hbm, out_ref,
    pbuf, hbuf, lhs, acc, pc_ref, hr_ref, keep_ref, send_sem, recv_sem, own_sem,
):
    row, col = lax.axis_index("row"), lax.axis_index("col")
    x, yh = row // NYH, row % NYH
    z, yl, core = col // 4, (col // 2) % 2, col % 2
    sign = 1 - 2 * core

    def wrap(value, size):
        value = jnp.where(value < 0, value + size, value)
        return jnp.where(value >= size, value - size, value)

    z_base = {dz: wrap(z + sign * dz, NZ) * 4 for dz in range(-6, 6)}
    z_base[6] = z_base[-6]
    in_chip = {(p, c): (1 - yl if p else yl) * 2 + (1 - core if c else core) for p in (0, 1) for c in (0, 1)}
    x_base = {dx: wrap(x + sign * dx, NX) * NYH for dx in range(-2, 2)}
    y_at = {dy: wrap(yh + sign * dy, NYH) for dy in range(-2, 2)}

    def col_of(dz, flip_pair, flip_core):
        return z_base[dz] + in_chip[int(flip_pair), int(flip_core)]

    def row_of(dx, dy):
        return x_base[dx] + y_at[dy]

    links = {
        "zp": (row, col_of(1, False, False)),
        "zm": (row, col_of(-1, False, False)),
        "y": (row, col_of(0, True, False)),
        "m": (row, col_of(0, False, True)),
        "xp": (row_of(1, 0), col),
        "xm": (row_of(-1, 0), col),
        "hp": (row_of(0, 1), col),
        "hm": (row_of(0, -1), col),
    }
    head, tail = pl.ds(0, SPLIT), pl.ds(SPLIT, FULL - SPLIT)

    def region(event):
        kind, d = event[0], event[1]
        if kind == "H":
            return hbuf.at[row_of(d, event[2])]
        if kind == "E":
            return pbuf.at[col_of(d, False, False), tail]
        if kind == "G":
            return pbuf.at[col_of(d, False, False), head]
        if kind == "A":
            return pbuf.at[col_of(d, True, False), head]
        if kind == "B":
            return pbuf.at[col_of(d, True, False), tail]
        if kind == "M":
            return pbuf.at[col_of(-d, False, True)]
        return pbuf.at[col_of(-d, True, True)]

    barrier = pltpu.get_barrier_semaphore()
    for device in links.values():
        pl.semaphore_signal(barrier, inc=1, device_id=device, device_id_type=MESH)

    own = [
        pltpu.make_async_copy(pc_hbm, pc_ref, own_sem.at[0]),
        pltpu.make_async_copy(hr_hbm, hr_ref, own_sem.at[1]),
        pltpu.make_async_copy(keep_hbm, keep_ref, own_sem.at[2]),
        pltpu.make_async_copy(p_ref, pbuf.at[col, pl.ds(0, ROWS)], own_sem.at[3]),
        pltpu.make_async_copy(h_ref, hbuf.at[row, pl.ds(0, ROWS)], own_sem.at[4]),
    ]
    for copy in own:
        copy.start()
    acc[...] = jnp.zeros_like(acc)
    own[0].wait()
    own[1].wait()
    line = lax.broadcasted_iota(jnp.int32, (META, BS), 0)
    p_meta = jnp.zeros((META, BS), jnp.int32)
    h_meta = jnp.zeros((META, BS), jnp.int32)
    base = 48 * (col // 3)
    for i in range(4):
        value = pc_ref[0, i]
        p_meta = jnp.where(line // 4 == i, jnp.where(value < 0, -1, value - base), p_meta)
        value = hr_ref[i // 2, i % 2]
        h_meta = jnp.where(line % 4 == i, jnp.where(value < 0, -2, value - 48 * row), h_meta)
    pbuf[col, pl.ds(ROWS, META), :] = p_meta.astype(jnp.float32).astype(jnp.bfloat16)
    hbuf[row, pl.ds(ROWS, META), :] = h_meta.astype(jnp.float32).astype(jnp.bfloat16)
    for copy in own[2:]:
        copy.wait()
    pl.semaphore_wait(barrier, len(links))

    sent = []

    def send(link, source, event):
        copy = pltpu.make_async_remote_copy(
            src_ref=source,
            dst_ref=source,
            send_sem=send_sem.at[len(sent)],
            recv_sem=recv_sem.at[sem_index(event)],
            device_id=links[link],
            device_id_type=MESH,
        )
        copy.start()
        sent.append(copy)

    def receive(event):
        here = region(event)
        pltpu.make_async_remote_copy(
            src_ref=here,
            dst_ref=here,
            send_sem=send_sem.at[0],
            recv_sem=recv_sem.at[sem_index(event)],
            device_id=links["m"],
            device_id_type=MESH,
        ).wait_recv()
        return here

    own_part = {"A": pbuf.at[col, head], "G": pbuf.at[col, head], "B": pbuf.at[col, tail], "E": pbuf.at[col, tail]}
    own_part.update({"M": pbuf.at[col], "H": hbuf.at[row]})
    for link, event in FIRST:
        send(link, own_part[event[0]], event)

    def block_row(r):
        h_tags = hbuf[r, pl.ds(ROWS, META), :].astype(jnp.float32)
        tags = []
        for u in range(3):
            p_tags = pbuf[3 * r + u, pl.ds(ROWS, META), :].astype(jnp.float32)
            tags.append(jnp.where(p_tags == h_tags, 1.0, 0.0))
        left = [[[None, None] for _ in range(4)] for _ in range(2)]
        for i in range(4):
            blocks = [pbuf[3 * r + u, pl.ds(i * BS, BS), :].reshape(8, META, BS) for u in range(3)]
            for q in range(4):
                picked = jnp.zeros_like(blocks[0])
                for u in range(3):
                    tag = jnp.broadcast_to(tags[u][4 * i + q : 4 * i + q + 1, :], (META, BS))
                    hit = jnp.broadcast_to(tag.astype(jnp.bfloat16)[None], (8, META, BS)) > 0
                    picked = jnp.where(hit, blocks[u], picked)
                left[q % 2][i][q // 2] = picked.reshape(BS, BS)
        right = [
            jnp.concatenate([hbuf[r, pl.ds(j * BS, BS), :], hbuf[r, pl.ds((2 + j) * BS, BS), :]], axis=0)
            for j in range(2)
        ]
        for m in range(2):
            sums = []
            for j in range(2):
                rows = jnp.concatenate([jnp.concatenate(v, axis=1) for v in left[j][2 * m : 2 * m + 2]], axis=0)
                sums.append(jnp.dot(rows, right[j], preferred_element_type=jnp.float32))
            for j in range(2):
                acc[j, pl.ds(m * 2 * BS, 2 * BS), :] += sums[j]

    def edges(s):
        return (4 * (z + NZ - s) + 2) // 3, (4 * (z + NZ + s + 1)) // 3

    def multiply(reach, before):
        if before is not None and before[1] == reach[1] == 2:
            first, last = edges(reach[0]), edges(before[0])
            if reach[0] == 6:
                spans = [(last[1], last[0] + NX * NYH)]
            else:
                spans = [(first[0], last[0]), (last[1], first[1])]
            for span in spans:
                lax.fori_loop(span[0], span[1], lambda r, carry: block_row(r % (NX * NYH)) or carry, 0)
            return

        def one(r, carry):
            dz = jnp.int32(0)
            for c in (3 * r, 3 * r + 2):
                d = (sign * (c // 4 - z) + NZ + 6) % NZ - 6
                dz = jnp.maximum(dz, jnp.maximum(d, -d))
            d = (r // NYH - x + NX) % NX
            dx = jnp.minimum(d, NX - d)
            now = (dz <= reach[0]) & (dx <= reach[1])
            if before is not None:
                now = now & ((dz > before[0]) | (dx > before[1]))
            pl.when(now)(lambda: block_row(r))
            return carry

        lax.fori_loop(0, NX * NYH, one, 0)

    reached = None
    have = set()
    retired = 0
    for event in ORDER:
        kind, d = event[0], event[1]
        if kind == "C":
            multiply(event[1:], reached)
            reached = event[1:]
            continue
        here = receive(event)
        have.add(event if kind == "H" else (kind, d % 12))
        if kind in "EGA":
            low, high = (-5, 6) if kind == "A" else (-6, 5)
            if low < d <= 0:
                send("zp", here, (kind, d - 1))
            if 0 <= d < high:
                send("zm", here, (kind, d + 1))
        if kind == "E":
            send("y", here, ("B", d))
        if kind in "EG" and ("E", d % 12) in have and ("G", d % 12) in have:
            send("m", pbuf.at[col_of(d, False, False)], ("M", d))
        if kind in "AB" and ("A", d % 12) in have and ("B", d % 12) in have:
            send("m", pbuf.at[col_of(d, True, False)], ("N", d))
        if kind == "H":
            dy = event[2]
            if d == 0:
                if dy == -1:
                    send("hp", here, ("H", 0, -2))
                send("xp", here, ("H", -1, dy))
                send("xm", here, ("H", 1, dy))
            elif d == -1:
                send("xp", here, ("H", -2, dy))
        while retired < len(sent) - LAG:
            sent[retired].wait_send()
            retired += 1

    for i in range(4):
        for j in range(2):
            total = acc[j, pl.ds(i * BS, BS), :]
            kept = jnp.where(keep_ref[j, i] == 1, total, jnp.zeros_like(total))
            out_ref[i, j] = kept.astype(out_ref.dtype)
    for copy in sent[retired:]:
        copy.wait_send()


def shards(p_blocks, p_cols, h_blocks, h_rows, keep):
    hbm = pl.BlockSpec(memory_space=pltpu.HBM)
    return pl.pallas_call(
        kernel,
        out_shape=jax.ShapeDtypeStruct((4, 2, BS, BS), jnp.bfloat16),
        in_specs=[hbm] * 5,
        out_specs=pl.BlockSpec(memory_space=pltpu.VMEM),
        scratch_shapes=[
            pltpu.VMEM((NZ * 4, FULL, BS), jnp.bfloat16),
            pltpu.VMEM((NX * NYH, FULL, BS), jnp.bfloat16),
            pltpu.VMEM((2, ROWS, 2 * BS), jnp.bfloat16),
            pltpu.VMEM((2, ROWS, BS), jnp.float32),
            pltpu.SMEM((1, 4), jnp.int32),
            pltpu.SMEM((2, 2), jnp.int32),
            pltpu.SMEM((2, 4), jnp.int32),
            pltpu.SemaphoreType.DMA((96,)),
            pltpu.SemaphoreType.DMA((SEMS,)),
            pltpu.SemaphoreType.DMA((5,)),
        ],
        compiler_params=pltpu.CompilerParams(
            collective_id=0, has_side_effects=True, vmem_limit_bytes=24 * 1024 * 1024
        ),
        name="filtered_product",
    )(*[
        pltpu.with_memory_space_constraint(array, pltpu.HBM)
        for array in (p_blocks.reshape(ROWS, BS), p_cols.reshape(1, 4), h_blocks.reshape(ROWS, BS), h_rows, keep.T)
    ])


def solution(mesh):
    return jax.shard_map(
        shards,
        mesh=mesh,
        in_specs=(
            P("row", "col", None, None),
            P("row", "col"),
            P("row", "col", None, None),
            P("row", "col"),
            P("row", "col"),
        ),
        out_specs=P("row", "col", None, None),
        check_vma=False,
    )
```

```python
import jax
import jax.numpy as jnp
from jax import lax
from jax.experimental import pallas as pl
from jax.experimental.pallas import tpu as pltpu
from jax.sharding import PartitionSpec as P

BS = 128
NX, NYH, NZ, NYL, NC = 4, 4, 12, 2, 2
ROWS = 4 * BS
META = 16
FULL = ROWS + META
SPLIT = 256
LAG = 42
MESH = pl.DeviceIdType.MESH

ORDER = [
    ("M", 0), ("E", -1), ("A", 0), ("E", 1), ("H", -1, 0), ("G", -1), ("G", 1), ("H", 1, 0), ("M", -1),
    ("E", -2), ("M", 1), ("A", -1), ("H", 0, -1), ("A", 1), ("H", -2, 0), ("E", 2), ("G", -2), ("G", 2),
    ("H", 0, 1), ("M", -2), ("E", -3), ("B", 0), ("M", 2), ("A", -2), ("H", -1, -1), ("A", 2), ("N", 0),
    ("B", -1), ("E", 3), ("H", 1, -1), ("G", -3), ("N", -1), ("G", 3), ("B", 1), ("H", -1, 1), ("M", -3),
    ("E", -4), ("A", -3), ("M", 3), ("H", 1, 1), ("B", -2), ("N", 1), ("A", 3), ("E", 4), ("H", -2, -1),
    ("N", -2), ("G", -4), ("G", 4), ("H", -2, 1), ("M", -4), ("E", -5), ("H", 0, -2), ("M", 4), ("A", -4),
    ("B", 2), ("A", 4), ("C", 1, 0), ("E", 5), ("N", 2), ("B", -3), ("G", -5), ("C", 2, 0), ("G", 5),
    ("B", 3), ("N", -3), ("H", -1, -2), ("M", -5), ("E", -6), ("A", -5), ("M", 5), ("N", 3), ("B", -4),
    ("H", 1, -2), ("A", 5), ("C", 3, 1), ("G", -6), ("N", -4), ("B", 4), ("H", -2, -2), ("B", -5), ("A", 6),
    ("C", 3, 2), ("M", -6), ("B", 5), ("N", 4), ("N", -5), ("C", 4, 2), ("B", -6), ("N", 5), ("C", 5, 2),
    ("N", -6), ("C", 6, 2),
]
FIRST = [
    ("y", ("A", 0)),
    ("zp", ("E", -1)),
    ("zm", ("E", 1)),
    ("zp", ("G", -1)),
    ("zm", ("G", 1)),
    ("hp", ("H", 0, -1)),
    ("hm", ("H", 0, 1)),
    ("xp", ("H", -1, 0)),
    ("xm", ("H", 1, 0)),
    ("y", ("B", 0)),
    ("m", ("M", 0)),
]
KINDS = {"E": 0, "A": 12, "B": 24, "M": 36, "N": 48, "G": 60}
SEMS = 88


def sem_index(event):
    if event[0] == "H":
        return 72 + (event[1] % 4) * 4 + event[2] % 4
    return KINDS[event[0]] + event[1] % 12


def kernel(
    p_ref, pc_hbm, h_ref, hr_hbm, keep_hbm, out_ref,
    pbuf, hbuf, lhs, acc, pc_ref, hr_ref, keep_ref, send_sem, recv_sem, own_sem,
):
    row, col = lax.axis_index("row"), lax.axis_index("col")
    x, yh = row // NYH, row % NYH
    z, yl, core = col // 4, (col // 2) % 2, col % 2
    sign = 1 - 2 * core

    def wrap(value, size):
        value = jnp.where(value < 0, value + size, value)
        return jnp.where(value >= size, value - size, value)

    z_base = {dz: wrap(z + sign * dz, NZ) * 4 for dz in range(-6, 6)}
    z_base[6] = z_base[-6]
    in_chip = {(p, c): (1 - yl if p else yl) * 2 + (1 - core if c else core) for p in (0, 1) for c in (0, 1)}
    x_base = {dx: wrap(x + sign * dx, NX) * NYH for dx in range(-2, 2)}
    y_at = {dy: wrap(yh + sign * dy, NYH) for dy in range(-2, 2)}

    def col_of(dz, flip_pair, flip_core):
        return z_base[dz] + in_chip[int(flip_pair), int(flip_core)]

    def row_of(dx, dy):
        return x_base[dx] + y_at[dy]

    links = {
        "zp": (row, col_of(1, False, False)),
        "zm": (row, col_of(-1, False, False)),
        "y": (row, col_of(0, True, False)),
        "m": (row, col_of(0, False, True)),
        "xp": (row_of(1, 0), col),
        "xm": (row_of(-1, 0), col),
        "hp": (row_of(0, 1), col),
        "hm": (row_of(0, -1), col),
    }
    head, tail = pl.ds(0, SPLIT), pl.ds(SPLIT, FULL - SPLIT)

    def region(event):
        kind, d = event[0], event[1]
        if kind == "H":
            return hbuf.at[row_of(d, event[2])]
        if kind == "E":
            return pbuf.at[col_of(d, False, False), tail]
        if kind == "G":
            return pbuf.at[col_of(d, False, False), head]
        if kind == "A":
            return pbuf.at[col_of(d, True, False), head]
        if kind == "B":
            return pbuf.at[col_of(d, True, False), tail]
        if kind == "M":
            return pbuf.at[col_of(-d, False, True)]
        return pbuf.at[col_of(-d, True, True)]

    barrier = pltpu.get_barrier_semaphore()
    for device in links.values():
        pl.semaphore_signal(barrier, inc=1, device_id=device, device_id_type=MESH)

    own = [
        pltpu.make_async_copy(pc_hbm, pc_ref, own_sem.at[0]),
        pltpu.make_async_copy(hr_hbm, hr_ref, own_sem.at[1]),
        pltpu.make_async_copy(keep_hbm, keep_ref, own_sem.at[2]),
        pltpu.make_async_copy(p_ref, pbuf.at[col, pl.ds(0, ROWS)], own_sem.at[3]),
        pltpu.make_async_copy(h_ref, hbuf.at[row, pl.ds(0, ROWS)], own_sem.at[4]),
    ]
    for copy in own:
        copy.start()
    acc[...] = jnp.zeros_like(acc)
    own[0].wait()
    own[1].wait()
    line = lax.broadcasted_iota(jnp.int32, (META, BS), 0)
    p_meta = jnp.zeros((META, BS), jnp.int32)
    h_meta = jnp.zeros((META, BS), jnp.int32)
    base = 48 * (col // 3)
    for i in range(4):
        value = pc_ref[0, i]
        p_meta = jnp.where(line // 4 == i, jnp.where(value < 0, -1, value - base), p_meta)
        value = hr_ref[i // 2, i % 2]
        h_meta = jnp.where(line % 4 == i, jnp.where(value < 0, -2, value - 48 * row), h_meta)
    pbuf[col, pl.ds(ROWS, META), :] = p_meta.astype(jnp.float32).astype(jnp.bfloat16)
    hbuf[row, pl.ds(ROWS, META), :] = h_meta.astype(jnp.float32).astype(jnp.bfloat16)
    for copy in own[2:]:
        copy.wait()
    pl.semaphore_wait(barrier, len(links))

    sent = []

    def send(link, source, event):
        copy = pltpu.make_async_remote_copy(
            src_ref=source,
            dst_ref=source,
            send_sem=send_sem.at[len(sent)],
            recv_sem=recv_sem.at[sem_index(event)],
            device_id=links[link],
            device_id_type=MESH,
        )
        copy.start()
        sent.append(copy)

    def receive(event):
        here = region(event)
        pltpu.make_async_remote_copy(
            src_ref=here,
            dst_ref=here,
            send_sem=send_sem.at[0],
            recv_sem=recv_sem.at[sem_index(event)],
            device_id=links["m"],
            device_id_type=MESH,
        ).wait_recv()
        return here

    own_part = {"A": pbuf.at[col, head], "G": pbuf.at[col, head], "B": pbuf.at[col, tail], "E": pbuf.at[col, tail]}
    own_part.update({"M": pbuf.at[col], "H": hbuf.at[row]})
    for link, event in FIRST:
        send(link, own_part[event[0]], event)

    def block_row(r):
        h_tags = hbuf[r, pl.ds(ROWS, META), :].astype(jnp.float32)
        tags = []
        for u in range(3):
            p_tags = pbuf[3 * r + u, pl.ds(ROWS, META), :].astype(jnp.float32)
            tags.append(jnp.where(p_tags == h_tags, 1.0, 0.0))
        left = [[[None, None] for _ in range(4)] for _ in range(2)]
        for i in range(4):
            blocks = [pbuf[3 * r + u, pl.ds(i * BS, BS), :].reshape(8, META, BS) for u in range(3)]
            for q in range(4):
                picked = jnp.zeros_like(blocks[0])
                for u in range(3):
                    tag = jnp.broadcast_to(tags[u][4 * i + q : 4 * i + q + 1, :], (META, BS))
                    hit = jnp.broadcast_to(tag.astype(jnp.bfloat16)[None], (8, META, BS)) > 0
                    picked = jnp.where(hit, blocks[u], picked)
                left[q % 2][i][q // 2] = picked.reshape(BS, BS)
        right = [
            jnp.concatenate([hbuf[r, pl.ds(j * BS, BS), :], hbuf[r, pl.ds((2 + j) * BS, BS), :]], axis=0)
            for j in range(2)
        ]
        for m in range(2):
            sums = []
            for j in range(2):
                rows = jnp.concatenate([jnp.concatenate(v, axis=1) for v in left[j][2 * m : 2 * m + 2]], axis=0)
                sums.append(jnp.dot(rows, right[j], preferred_element_type=jnp.float32))
            for j in range(2):
                acc[j, pl.ds(m * 2 * BS, 2 * BS), :] += sums[j]

    def edges(s):
        return (4 * (z + NZ - s) + 2) // 3, (4 * (z + NZ + s + 1)) // 3

    def multiply(reach, before):
        if before is not None and before[1] == reach[1] == 2:
            first, last = edges(reach[0]), edges(before[0])
            if reach[0] == 6:
                spans = [(last[1], last[0] + NX * NYH)]
            else:
                spans = [(first[0], last[0]), (last[1], first[1])]
            for span in spans:
                lax.fori_loop(span[0], span[1], lambda r, carry: block_row(r % (NX * NYH)) or carry, 0)
            return

        def one(r, carry):
            dz = jnp.int32(0)
            for c in (3 * r, 3 * r + 2):
                d = (sign * (c // 4 - z) + NZ + 6) % NZ - 6
                dz = jnp.maximum(dz, jnp.maximum(d, -d))
            d = (r // NYH - x + NX) % NX
            dx = jnp.minimum(d, NX - d)
            now = (dz <= reach[0]) & (dx <= reach[1])
            if before is not None:
                now = now & ((dz > before[0]) | (dx > before[1]))
            pl.when(now)(lambda: block_row(r))
            return carry

        lax.fori_loop(0, NX * NYH, one, 0)

    reached = None
    have = set()
    retired = 0
    for place, event in enumerate(ORDER):
        kind, d = event[0], event[1]
        if kind == "C":
            multiply(event[1:], reached)
            reached = event[1:]
            continue
        here = receive(event)
        have.add(event if kind == "H" else (kind, d % 12))
        if kind in "EGA":
            low, high = (-5, 6) if kind == "A" else (-6, 5)
            if low < d <= 0:
                send("zp", here, (kind, d - 1))
            if 0 <= d < high:
                send("zm", here, (kind, d + 1))
        if kind == "E":
            send("y", here, ("B", d))
        if kind in "EG" and ("E", d % 12) in have and ("G", d % 12) in have:
            send("m", pbuf.at[col_of(d, False, False)], ("M", d))
        if kind in "AB" and ("A", d % 12) in have and ("B", d % 12) in have:
            send("m", pbuf.at[col_of(d, True, False)], ("N", d))
        if kind == "H":
            dy = event[2]
            if d == 0:
                if dy == -1:
                    send("hp", here, ("H", 0, -2))
                send("xp", here, ("H", -1, dy))
                send("xm", here, ("H", 1, dy))
            elif d == -1:
                send("xp", here, ("H", -2, dy))
        while retired < len(sent) - (LAG if place < len(ORDER) - 8 else 12):
            sent[retired].wait_send()
            retired += 1

    for i in range(4):
        for j in range(2):
            total = acc[j, pl.ds(i * BS, BS), :]
            kept = jnp.where(keep_ref[j, i] == 1, total, jnp.zeros_like(total))
            out_ref[i, j] = kept.astype(out_ref.dtype)
    for copy in sent[retired:]:
        copy.wait_send()


def shards(p_blocks, p_cols, h_blocks, h_rows, keep):
    hbm = pl.BlockSpec(memory_space=pltpu.HBM)
    return pl.pallas_call(
        kernel,
        out_shape=jax.ShapeDtypeStruct((4, 2, BS, BS), jnp.bfloat16),
        in_specs=[hbm] * 5,
        out_specs=pl.BlockSpec(memory_space=pltpu.VMEM),
        scratch_shapes=[
            pltpu.VMEM((NZ * 4, FULL, BS), jnp.bfloat16),
            pltpu.VMEM((NX * NYH, FULL, BS), jnp.bfloat16),
            pltpu.VMEM((2, ROWS, 2 * BS), jnp.bfloat16),
            pltpu.VMEM((2, ROWS, BS), jnp.float32),
            pltpu.SMEM((1, 4), jnp.int32),
            pltpu.SMEM((2, 2), jnp.int32),
            pltpu.SMEM((2, 4), jnp.int32),
            pltpu.SemaphoreType.DMA((96,)),
            pltpu.SemaphoreType.DMA((SEMS,)),
            pltpu.SemaphoreType.DMA((5,)),
        ],
        compiler_params=pltpu.CompilerParams(
            collective_id=0, has_side_effects=True, vmem_limit_bytes=24 * 1024 * 1024
        ),
        name="filtered_product",
    )(*[
        pltpu.with_memory_space_constraint(array, pltpu.HBM)
        for array in (p_blocks.reshape(ROWS, BS), p_cols.reshape(1, 4), h_blocks.reshape(ROWS, BS), h_rows, keep.T)
    ])


def solution(mesh):
    return jax.shard_map(
        shards,
        mesh=mesh,
        in_specs=(
            P("row", "col", None, None),
            P("row", "col"),
            P("row", "col", None, None),
            P("row", "col"),
            P("row", "col"),
        ),
        out_specs=P("row", "col", None, None),
        check_vma=False,
    )
```
